32 devices in a mesh: pair: 2 (over y), virt: 16 (over z, x, core).
Axes of the slice: x: 2, y: 2, z: 4, core: 2. Of those that a mesh axis runs over, the one named last changes fastest.
Arguments:
- amplitudes: bfloat16 [2048, 65536], P('pair', 'virt'), may hold values from -6 to 6
- integrals: bfloat16 [65536, 1024], P('virt', 'pair'), may hold values from -0.0234375 to 0.0234375
- occ_pairs: int32 [2048, 2], P(('pair', 'virt')), may hold values from 0 to 95, as said below
- partners: int32 [2048], P(('pair', 'virt')), may hold values from 0 to 2047, as said below
- virt_list: int32 [32], replicated, may hold values from 0 to 511
- eps_occ: float32 [96], replicated, may hold values from -2 to -0.5
- eps_virt: float32 [512], replicated, may hold values from 0.2 to 3
Outputs:
- update: float32 [2048, 1024], P(('pair', 'virt'))
The draws below stay inside these ranges and needn't reach their ends.
Inputs may be any that keep to these rules, and one draw needn't show every extreme that they name: Row r holds the pair (i, j) with i != j; row partners[r] holds (j, i), partners[partners[r]] = r, and partners[r] lies in the same index of pair and in the index of virt 16 / 2 away under the placement of the output rows. `occ_pairs`: the two orbitals of a row differ.
All inputs are finite; a program needn't handle non-finite values.
Results may differ from the reference program's by a relative error of at most 0.0003.
Values may be sent and summed in bfloat16 or wider, within the bound.
No kernel may reach another device: no remote copies, remote signals or barrier semaphores. Data moves between devices by JAX's collectives and lax.ppermute only.
A program may use at most 192 MiB of HBM per device.

```python
import jax
import jax.numpy as jnp

NV = 512
NO = 96
W = 32
OP_DEV = 1024
CD = 65536
AB = 1024
OPAIRS = 2048
N_PAIR = 2
N_VIRT = 16


def pair_tables(key):
    base_key = jax.random.fold_in(key, 11)
    key_first, key_second, key_perm = jax.random.split(base_key, 3)
    rows = OP_DEV // N_VIRT
    half = N_VIRT // 2
    first = jax.random.randint(key_first, (N_PAIR, half, rows), 0, NO).astype(jnp.int32)
    second = ((first + jax.random.randint(key_second, (N_PAIR, half, rows), 1, NO)) % NO).astype(jnp.int32)
    sigma = jax.vmap(lambda s: jax.random.permutation(s, rows))(jax.random.split(key_perm, N_PAIR * half))
    sigma = sigma.reshape(N_PAIR, half, rows).astype(jnp.int32)
    inverse = jnp.argsort(sigma, axis=-1).astype(jnp.int32)
    high_first = jnp.take_along_axis(second, inverse, axis=-1)
    high_second = jnp.take_along_axis(first, inverse, axis=-1)
    low_pairs = jnp.stack([first, second], axis=-1)
    high_pairs = jnp.stack([high_first, high_second], axis=-1)
    occ = jnp.concatenate([low_pairs, high_pairs], axis=1).reshape(OPAIRS, 2)
    block_base = (jnp.arange(N_PAIR, dtype=jnp.int32) * OP_DEV)[:, None, None]
    low_virt = jnp.arange(half, dtype=jnp.int32)[None, :, None]
    low_partner = block_base + (low_virt + half) * rows + sigma
    high_partner = block_base + low_virt * rows + inverse
    partner = jnp.concatenate([low_partner, high_partner], axis=1).reshape(OPAIRS)
    return (occ.astype(jnp.int32), partner.astype(jnp.int32))


def draw_occ_pairs(key, part):
    return pair_tables(key)[0]


def draw_partners(key, part):
    return pair_tables(key)[1]


def set_ends(result, key, low, high):
    place = [jax.random.randint(jax.random.fold_in(key, axis), (), 0, length) for axis, length in enumerate(result.shape)]
    main_axis = result.shape.index(max(result.shape))
    next_to = place[:main_axis] + [(place[main_axis] + 1) % result.shape[main_axis]] + place[main_axis + 1:]
    return result.at[tuple(place)].set(low).at[tuple(next_to)].set(high)


def spiked(entries, key, source, target, blocks, factor):
    owner, partner = [(jnp.arange(entries.shape[dim]) // (entries.shape[dim] // blocks)).reshape([-1 if axis == dim else 1 for axis in range(entries.ndim)]) for dim in (source, target)]
    chosen = jax.random.permutation(key, blocks)[partner]
    strong = (owner == chosen) | (owner == (partner + blocks // 2) % blocks)
    return jnp.where(strong, factor * entries, entries)


def levels(rng, shape, cuts, least, high):
    loudness, own = 1.0, jax.random.fold_in(rng, 6)
    for position, blocks in cuts:
        draws = jnp.exp(jax.random.uniform(jax.random.fold_in(own, position), (blocks,), jnp.float32, least / len(cuts), high / len(cuts)))
        loudness = loudness * jnp.repeat(draws, shape[position] // blocks).reshape([-1 if axis == position else 1 for axis in range(len(shape))])
    return loudness


def bell_draw(rng, shape, deviation, limit, cuts=(), held_as=jnp.bfloat16):
    result = jax.random.normal(rng, shape, jnp.float32) * deviation
    if len(cuts) > 0:
        result = levels(rng, shape, cuts, -0.22, 0.18) * result
    return jnp.clip(result, min=-limit, max=limit).astype(held_as)


def gaussian_with(own_key, dims, width, reach, pieces, heavy, held_as=jnp.bfloat16):
    result = width * jax.random.normal(own_key, dims, jnp.float32)
    if pieces:
        result = result * levels(own_key, dims, pieces, -0.22, 0.18)
    return jnp.clip(spiked(result, jax.random.fold_in(own_key, 3), *heavy), -reach, reach).astype(held_as)


def setup_inputs(seed: int = 0) -> dict:
    splits = jax.random.split(jax.random.key(seed), 8)
    return {
        "amplitudes": gaussian_with(splits[0], (OPAIRS, CD), 1.0, 6.0, ((0, 2), (1, 16)), (1, 0, 16, 2.0)),
        "integrals": bell_draw(splits[1], (CD, AB), CD ** -0.5, 0.0234375, ((0, 16), (1, 2))),
        "occ_pairs": draw_occ_pairs(jax.random.fold_in(splits[7], 71), 0),
        "partners": draw_partners(jax.random.fold_in(splits[7], 71), 0),
        "virt_list": set_ends(jax.random.randint(splits[4], (W,), 0, NV), jax.random.fold_in(splits[4], 1), 0, NV - 1).astype(jnp.int32),
        "eps_occ": jnp.clip(jax.random.uniform(splits[5], (NO,), jnp.float32, -2.0, -0.5), -2.0, -0.5),
        "eps_virt": jnp.clip(jax.random.uniform(splits[6], (NV,), jnp.float32, 0.2, 3.0), 0.2, 3.0),
    }


def reference(amplitudes, integrals, occ_pairs, partners, virt_list, eps_occ, eps_virt):
    ladder = jnp.dot(amplitudes, integrals, preferred_element_type=jnp.float32)
    flipped = jnp.take(ladder, partners, axis=0)
    flipped = flipped.reshape(-1, W, W).transpose(0, 2, 1).reshape(-1, W * W)
    symmetric = ladder + flipped
    occ_sum = eps_occ[occ_pairs[:, 0]] + eps_occ[occ_pairs[:, 1]]
    virt_energy = eps_virt[virt_list]
    virt_sum = (virt_energy[:, None] + virt_energy[None, :]).reshape(-1)
    denominator = virt_sum[None, :] - occ_sum[:, None]
    return symmetric / denominator
```

```python
import jax
import jax.numpy as jnp
from jax import lax
from jax.sharding import PartitionSpec as P


def passed_along(value, axis, steps):
    count = lax.axis_size(axis)
    pairs = [(source, (source + steps) % count) for source in range(count)]
    return lax.ppermute(value, axis, pairs)


def transpose_block(values, width):
    count = values.shape[0]
    return values.reshape(count, width, width).transpose(0, 2, 1).reshape(count, width * width)


def column_cuts(columns):
    half, quarter = columns // 2, columns // 4
    return [(0, half), (half, half + quarter), (half + quarter, columns)]


def in_column_order(blocks, count):
    own = lax.axis_index("pair")
    ordered = []
    for place in range(count):
        block = blocks[place]
        for index in range(1, count):
            block = jnp.where(own == index, blocks[(place - index) % count], block)
        ordered.append(block)
    return jnp.concatenate(ordered, axis=1)


def per_device(amplitudes, integrals, occ_pairs, partners, virt_list, eps_occ, eps_virt):
    width = virt_list.shape[0]
    count = lax.axis_size("pair")
    half = lax.axis_size("virt") // 2
    cuts = column_cuts(integrals.shape[1])
    def multiplied(columns):
        return jnp.dot(amplitudes, columns, preferred_element_type=jnp.float32)

    def sent(low, high):
        return [passed_along(integrals[:, low:high], "pair", -shift) for shift in range(1, count)]

    def after(value, earlier):
        return lax.optimization_barrier((value, earlier))[0]

    def summed(partial_value):
        mine = lax.psum_scatter(partial_value, "virt", scatter_dimension=0, tiled=True)
        return mine, passed_along(mine, "virt", half)

    in_flight = [sent(*cuts[0])]
    own_product = multiplied(integrals)
    sums = [[summed(own_product)]] + [[] for _ in range(1, count)]
    integrals = after(integrals, own_product)
    in_flight.append(sent(*cuts[1]))
    last_product = own_product
    for step in range(len(cuts)):
        arrived = after(in_flight[step], last_product)
        products = [multiplied(piece) for piece in arrived]
        for shift in range(1, count):
            sums[shift].append(summed(products[shift - 1]))
        last_product = products
        if step + 2 < len(cuts):
            integrals = after(integrals, products)
            in_flight.append(sent(*cuts[step + 2]))

    mine = in_column_order([jnp.concatenate([m for m, _ in parts], axis=1) for parts in sums], count)
    other = in_column_order([jnp.concatenate([o for _, o in parts], axis=1) for parts in sums], count)

    flipped = jnp.take(other, partners % mine.shape[0], axis=0)
    total = mine + transpose_block(flipped, width)

    occ_ids = jnp.arange(eps_occ.shape[0], dtype=jnp.int32)
    occ_match = occ_pairs[:, :, None] == occ_ids[None, None, :]
    occ_sum = jnp.sum(jnp.where(occ_match, eps_occ[None, None, :], 0.0), axis=(1, 2))
    virt_ids = jnp.arange(eps_virt.shape[0], dtype=jnp.int32)
    virt_match = virt_list[:, None] == virt_ids[None, :]
    virt_energy = jnp.sum(jnp.where(virt_match, eps_virt[None, :], 0.0), axis=1)
    virt_sum = (virt_energy[:, None] + virt_energy[None, :]).reshape(-1)
    denominator = virt_sum[None, :] - occ_sum[:, None]
    return total / denominator


def solution(mesh):
    placed = (
        P("pair", "virt"),
        P("virt", "pair"),
        P(("pair", "virt"), None),
        P(("pair", "virt")),
        P(),
        P(),
        P(),
    )
    return jax.shard_map(
        per_device, mesh=mesh, in_specs=placed, out_specs=P(("pair", "virt"), None), check_vma=False
    )
```

```python
import jax
import jax.numpy as jnp
from jax import lax
from jax.sharding import PartitionSpec as P

INNER = 4


def passed_along(value, axis, steps):
    count = lax.axis_size(axis)
    pairs = [(source, (source + steps) % count) for source in range(count)]
    return lax.ppermute(value, axis, pairs)


def transpose_block(values, width):
    count = values.shape[0]
    return values.reshape(count, width, width).transpose(0, 2, 1).reshape(count, width * width)


def column_cuts(columns):
    half, quarter = columns // 2, columns // 4
    return [(0, half), (half, half + quarter), (half + quarter, columns)]


def after(value, earlier):
    return lax.optimization_barrier((value, earlier))[0]


def in_column_order(blocks, count):
    own = lax.axis_index("pair")
    ordered = []
    for place in range(count):
        block = blocks[place]
        for index in range(1, count):
            block = jnp.where(own == index, blocks[(place - index) % count], block)
        ordered.append(block)
    return jnp.concatenate(ordered, axis=1)


def exchanged_sum(partial_value):
    size = lax.axis_size("virt")
    outer = size // INNER
    rows = partial_value.shape[0] // size
    width = partial_value.shape[1]
    inner_groups = [[o * INNER + i for i in range(INNER)] for o in range(outer)]
    outer_groups = [[o * INNER + i for o in range(outer)] for i in range(INNER)]
    blocks = partial_value.reshape(2, outer // 2, INNER, rows, width).transpose(2, 1, 0, 3, 4)
    blocks = lax.all_to_all(blocks, "virt", 0, 0, axis_index_groups=inner_groups)
    blocks = jnp.sum(blocks, axis=0)
    blocks = jnp.concatenate([blocks, blocks], axis=0)
    blocks = lax.all_to_all(blocks, "virt", 0, 0, axis_index_groups=outer_groups)
    both = jnp.sum(blocks, axis=0)
    upper = lax.axis_index("virt") >= size // 2
    return jnp.where(upper, both[1], both[0]), jnp.where(upper, both[0], both[1])


def per_device(amplitudes, integrals, occ_pairs, partners, virt_list, eps_occ, eps_virt):
    width = virt_list.shape[0]
    count = lax.axis_size("pair")
    half = lax.axis_size("virt") // 2
    cuts = column_cuts(integrals.shape[1])

    def multiplied(columns):
        return jnp.dot(amplitudes, columns, preferred_element_type=jnp.float32)

    in_flight, source = [], integrals
    for low, high in cuts:
        piece = source[:, low:high]
        source = after(source, piece)
        in_flight.append([passed_along(piece, "pair", -shift) for shift in range(1, count)])

    own_sum = lax.psum_scatter(multiplied(source), "virt", scatter_dimension=0, tiled=True)
    sums = [[] for _ in range(count)]
    earlier = source
    for step, pieces in enumerate(in_flight):
        for shift in range(1, count):
            both = exchanged_sum(multiplied(after(pieces[shift - 1], earlier)))
            earlier = both[0]
            sums[shift].append(both)
        if step == 0:
            own_sum = after(own_sum, earlier)
            sums[0].append((own_sum, passed_along(own_sum, "virt", half)))

    mine = in_column_order([jnp.concatenate([m for m, _ in parts], axis=1) for parts in sums], count)
    other = in_column_order([jnp.concatenate([o for _, o in parts], axis=1) for parts in sums], count)

    flipped = jnp.take(other, partners % mine.shape[0], axis=0)
    total = mine + transpose_block(flipped, width)

    occ_ids = jnp.arange(eps_occ.shape[0], dtype=jnp.int32)
    occ_match = occ_pairs[:, :, None] == occ_ids[None, None, :]
    occ_sum = jnp.sum(jnp.where(occ_match, eps_occ[None, None, :], 0.0), axis=(1, 2))
    virt_ids = jnp.arange(eps_virt.shape[0], dtype=jnp.int32)
    virt_match = virt_list[:, None] == virt_ids[None, :]
    virt_energy = jnp.sum(jnp.where(virt_match, eps_virt[None, :], 0.0), axis=1)
    virt_sum = (virt_energy[:, None] + virt_energy[None, :]).reshape(-1)
    denominator = virt_sum[None, :] - occ_sum[:, None]
    return total / denominator


def solution(mesh):
    placed = (
        P("pair", "virt"),
        P("virt", "pair"),
        P(("pair", "virt"), None),
        P(("pair", "virt")),
        P(),
        P(),
        P(),
    )
    return jax.shard_map(
        per_device, mesh=mesh, in_specs=placed, out_specs=P(("pair", "virt"), None), check_vma=False
    )
```

```python
import functools

import jax
import jax.numpy as jnp
from jax import lax
from jax.experimental import pallas as pl
from jax.experimental.pallas import tpu as pltpu
from jax.sharding import PartitionSpec as P

INNER = 4
VMEM_BYTES = 20 * 1024 * 1024


def passed_along(value, axis, steps):
    count = lax.axis_size(axis)
    pairs = [(source, (source + steps) % count) for source in range(count)]
    return lax.ppermute(value, axis, pairs)


def transpose_block(values, width):
    count = values.shape[0]
    return values.reshape(count, width, width).transpose(0, 2, 1).reshape(count, width * width)


def column_cuts(columns):
    part = columns // 4
    return [(low, low + part) for low in range(0, columns, part)]


def after(value, earlier):
    return lax.optimization_barrier((value, earlier))[0]


def in_column_order(blocks, count):
    own = lax.axis_index("pair")
    ordered = []
    for place in range(count):
        block = blocks[place]
        for index in range(1, count):
            block = jnp.where(own == index, blocks[(place - index) % count], block)
        ordered.append(block)
    return jnp.concatenate(ordered, axis=1)


def product_kernel(steps, outer, inner_ref, a_ref, b_ref, *refs):
    out_refs, total_ref = refs[:-1], refs[-1]
    step = pl.program_id(0)
    term = jnp.dot(a_ref[...], b_ref[...], preferred_element_type=jnp.float32)

    @pl.when(step == 0)
    def _():
        total_ref[...] = term

    @pl.when(step > 0)
    def _():
        total_ref[...] += term

    @pl.when(step == steps - 1)
    def _():
        rows = total_ref.shape[0] // (outer * INNER)
        for t, out_ref in enumerate(out_refs):
            inner = inner_ref[0] ^ t
            for place in range(outer):
                block = ((place % 2) * (outer // 2) + place // 2) * INNER + inner
                start = pl.multiple_of(block * rows, rows)
                out_ref[place * rows : (place + 1) * rows, :] = total_ref[pl.ds(start, rows), :]


def multiplied(amplitudes, columns, inner, outer):
    rows, depth = amplitudes.shape
    width = columns.shape[1]
    steps = 8
    part = depth // steps
    shape = jax.ShapeDtypeStruct((rows // INNER, width), jnp.float32)
    return pl.pallas_call(
        functools.partial(product_kernel, steps, outer),
        grid=(steps,),
        out_shape=[shape] * INNER,
        in_specs=[
            pl.BlockSpec(memory_space=pltpu.SMEM),
            pl.BlockSpec((rows, part), lambda k: (0, k)),
            pl.BlockSpec((part, width), lambda k: (k, 0)),
        ],
        out_specs=[pl.BlockSpec(shape.shape, lambda k: (0, 0))] * INNER,
        scratch_shapes=[pltpu.VMEM((rows, width), jnp.float32)],
        compiler_params=pltpu.CompilerParams(vmem_limit_bytes=VMEM_BYTES),
        cost_estimate=pl.CostEstimate(flops=0, bytes_accessed=0, transcendentals=0),
    )(inner, amplitudes, columns)


def blocked_kernel(steps, blocks, a_ref, b_ref, out_ref, total_ref):
    step = pl.program_id(0)
    term = jnp.dot(a_ref[...], b_ref[...], preferred_element_type=jnp.float32)

    @pl.when(step == 0)
    def _():
        total_ref[...] = term

    @pl.when(step > 0)
    def _():
        total_ref[...] += term

    @pl.when(step == steps - 1)
    def _():
        rows = out_ref.shape[1]
        for place, block in enumerate(blocks):
            out_ref[place] = total_ref[block * rows : (block + 1) * rows, :]


def blocked_product(amplitudes, columns, blocks):
    rows, depth = amplitudes.shape
    width = columns.shape[1]
    steps = 8
    part = depth // steps
    shape = jax.ShapeDtypeStruct((len(blocks), rows // len(blocks), width), jnp.float32)
    return pl.pallas_call(
        functools.partial(blocked_kernel, steps, blocks),
        grid=(steps,),
        out_shape=shape,
        in_specs=[
            pl.BlockSpec((rows, part), lambda k: (0, k)),
            pl.BlockSpec((part, width), lambda k: (k, 0)),
        ],
        out_specs=pl.BlockSpec(shape.shape, lambda k: (0, 0, 0)),
        scratch_shapes=[pltpu.VMEM((rows, width), jnp.float32)],
        compiler_params=pltpu.CompilerParams(vmem_limit_bytes=VMEM_BYTES),
        cost_estimate=pl.CostEstimate(flops=0, bytes_accessed=0, transcendentals=0),
    )(amplitudes, columns)


def grouped_sum(product, outer):
    size, rows, width = product.shape
    inner_groups = [[o * INNER + i for i in range(INNER)] for o in range(outer)]
    outer_groups = [[o * INNER + i for o in range(outer)] for i in range(INNER)]
    blocks = product.reshape(INNER, outer * rows, width)
    blocks = lax.all_to_all(blocks, "virt", 0, 0, axis_index_groups=inner_groups)
    blocks = jnp.sum(blocks, axis=0).reshape(outer // 2, 2 * rows, width)
    blocks = jnp.concatenate([blocks, blocks], axis=0)
    blocks = lax.all_to_all(blocks, "virt", 0, 0, axis_index_groups=outer_groups)
    return jnp.sum(blocks, axis=0)


def sum_kernel(outer, place_ref, *refs):
    ins, outs = refs[:INNER], refs[INNER:]
    rows = outs[0].shape[0]
    for d, out_ref in enumerate(outs):
        place = place_ref[0] ^ d
        own = pl.ds(pl.multiple_of(place * rows, rows), rows)
        out_ref[...] = (ins[0][own, :] + ins[1][own, :]) + (ins[2][own, :] + ins[3][own, :])


def summed_inner(terms, place, outer):
    rows, width = terms[0].shape
    shape = jax.ShapeDtypeStruct((2 * rows // outer, width), jnp.float32)
    return pl.pallas_call(
        functools.partial(sum_kernel, outer),
        out_shape=[shape] * (outer // 2),
        in_specs=[pl.BlockSpec(memory_space=pltpu.SMEM)] + [pl.BlockSpec(memory_space=pltpu.VMEM)] * INNER,
        out_specs=[pl.BlockSpec(memory_space=pltpu.VMEM)] * (outer // 2),
        compiler_params=pltpu.CompilerParams(vmem_limit_bytes=VMEM_BYTES),
        cost_estimate=pl.CostEstimate(flops=0, bytes_accessed=0, transcendentals=0),
    )(place, *terms)


def flipped_along(value, axis, bits):
    count = lax.axis_size(axis)
    return lax.ppermute(value, axis, [(source, source ^ bits) for source in range(count)])


def exchanged_sum(terms, place, outer, first=None):
    held = [terms[0]] + [flipped_along(terms[t], "virt", t) for t in range(1, INNER)]
    held, first = lax.optimization_barrier((held, first))
    parts = summed_inner(held, place, outer)
    total = parts[0]
    for t in range(1, outer):
        total = total + flipped_along(parts[t % (outer // 2)], "virt", t * INNER)
    return total


def per_device(amplitudes, integrals, occ_pairs, partners, virt_list, eps_occ, eps_virt):
    width = virt_list.shape[0]
    count = lax.axis_size("pair")
    size = lax.axis_size("virt")
    outer = size // INNER
    rows = amplitudes.shape[0] // size
    cuts = column_cuts(integrals.shape[1])
    me = lax.axis_index("virt")
    inner = (me % INNER).astype(jnp.int32).reshape(1)
    place = ((me // INNER) % (outer // 2)).astype(jnp.int32).reshape(1)

    def sent(piece):
        return [passed_along(piece, "pair", -shift) for shift in range(1, count)]

    first = integrals[:, cuts[0][0] : cuts[0][1]]
    rest = after(integrals, first)
    pieces = [first] + [rest[:, low:high] for low, high in cuts[1:]]
    in_flight = [sent(pieces[0]), sent(pieces[1])]
    exchange_order = [(h * (outer // 2) + o) * INNER + i for i in range(INNER) for o in range(outer // 2) for h in range(2)]
    own_product = blocked_product(amplitudes, after(rest, pieces), exchange_order)
    own_sum = grouped_sum(own_product, outer)
    sums = [[own_sum]] + [[] for _ in range(1, count)]
    upper = me >= size // 2
    earlier = own_product
    for step in range(len(cuts)):
        arrived, earlier = lax.optimization_barrier((in_flight[step], earlier))
        if step + 2 < len(cuts):
            in_flight.append(sent(after(pieces[step + 2], arrived)))
        for shift in range(1, count):
            product = multiplied(amplitudes, arrived[shift - 1], inner, outer)
            earlier = exchanged_sum(product, place, outer)
            sums[shift].append(earlier)

    both = in_column_order([jnp.concatenate(parts, axis=1) for parts in sums], count)
    mine = jnp.where(upper, both[rows:], both[:rows])
    other = jnp.where(upper, both[:rows], both[rows:])
    flipped = jnp.take(other, partners % mine.shape[0], axis=0)
    total = mine + transpose_block(flipped, width)

    occ_ids = jnp.arange(eps_occ.shape[0], dtype=jnp.int32)
    occ_match = occ_pairs[:, :, None] == occ_ids[None, None, :]
    occ_sum = jnp.sum(jnp.where(occ_match, eps_occ[None, None, :], 0.0), axis=(1, 2))
    virt_ids = jnp.arange(eps_virt.shape[0], dtype=jnp.int32)
    virt_match = virt_list[:, None] == virt_ids[None, :]
    virt_energy = jnp.sum(jnp.where(virt_match, eps_virt[None, :], 0.0), axis=1)
    virt_sum = (virt_energy[:, None] + virt_energy[None, :]).reshape(-1)
    denominator = virt_sum[None, :] - occ_sum[:, None]
    return total / denominator


def solution(mesh):
    placed = (
        P("pair", "virt"),
        P("virt", "pair"),
        P(("pair", "virt"), None),
        P(("pair", "virt")),
        P(),
        P(),
        P(),
    )
    return jax.shard_map(
        per_device, mesh=mesh, in_specs=placed, out_specs=P(("pair", "virt"), None), check_vma=False
    )
```

```python
import functools

import jax
import jax.numpy as jnp
from jax import lax
from jax.experimental import pallas as pl
from jax.experimental.pallas import tpu as pltpu
from jax.sharding import PartitionSpec as P

PRODUCT_BYTES = 51 * 1024 * 1024
SUM_BYTES = 8 * 1024 * 1024


def passed_along(value, axis, steps):
    count = lax.axis_size(axis)
    pairs = [(source, (source + steps) % count) for source in range(count)]
    return lax.ppermute(value, axis, pairs)


def transpose_block(values, width):
    count = values.shape[0]
    return values.reshape(count, width, width).transpose(0, 2, 1).reshape(count, width * width)


def column_cuts(columns):
    part = columns // 4
    return [(low, low + part) for low in range(0, columns, part)]


def after(value, earlier):
    return lax.optimization_barrier((value, earlier))[0]


def in_column_order(blocks, count):
    own = lax.axis_index("pair")
    ordered = []
    for place in range(count):
        block = blocks[place]
        for index in range(1, count):
            block = jnp.where(own == index, blocks[(place - index) % count], block)
        ordered.append(block)
    return jnp.concatenate(ordered, axis=1)


def product_kernel(steps, order, bit_ref, a_ref, b_ref, keep_ref, send_ref, total_ref):
    step = pl.program_id(0)
    term = jnp.dot(a_ref[...], b_ref[...], preferred_element_type=jnp.float32)

    @pl.when(step == 0)
    def _():
        total_ref[...] = term

    @pl.when(step > 0)
    def _():
        total_ref[...] += term

    @pl.when(step == steps - 1)
    def _():
        rows = keep_ref.shape[0] // len(order)
        for out_ref, bit in ((keep_ref, bit_ref[0]), (send_ref, 1 - bit_ref[0])):
            for place, block in enumerate(order):
                start = pl.multiple_of((block + bit) * rows, rows)
                out_ref[place * rows : (place + 1) * rows, :] = total_ref[pl.ds(start, rows), :]


def multiplied(amplitudes, columns, bit, order):
    rows, depth = amplitudes.shape
    width = columns.shape[1]
    steps = 4
    part = depth // steps
    shape = jax.ShapeDtypeStruct((rows // 2, width), jnp.float32)
    return pl.pallas_call(
        functools.partial(product_kernel, steps, order),
        grid=(steps,),
        out_shape=[shape] * 2,
        in_specs=[
            pl.BlockSpec(memory_space=pltpu.SMEM),
            pl.BlockSpec((rows, part), lambda k: (0, k)),
            pl.BlockSpec((part, width), lambda k: (k, 0)),
        ],
        out_specs=[pl.BlockSpec(shape.shape, lambda k: (0, 0))] * 2,
        scratch_shapes=[pltpu.VMEM((rows, width), jnp.float32)],
        compiler_params=pltpu.CompilerParams(vmem_limit_bytes=PRODUCT_BYTES),
        cost_estimate=pl.CostEstimate(flops=0, bytes_accessed=0, transcendentals=0),
    )(bit, amplitudes, columns)


def halve_kernel(bit_ref, mine_ref, came_ref, keep_ref, send_ref):
    rows = keep_ref.shape[0]
    for out_ref, bit in ((keep_ref, bit_ref[0]), (send_ref, 1 - bit_ref[0])):
        part = pl.ds(pl.multiple_of(bit * rows, rows), rows)
        out_ref[...] = mine_ref[part, :] + came_ref[part, :]


def halved(mine, came, bit):
    rows, width = mine.shape
    shape = jax.ShapeDtypeStruct((rows // 2, width), jnp.float32)
    return pl.pallas_call(
        halve_kernel,
        out_shape=[shape] * 2,
        in_specs=[pl.BlockSpec(memory_space=pltpu.SMEM)] + [pl.BlockSpec(memory_space=pltpu.VMEM)] * 2,
        out_specs=[pl.BlockSpec(memory_space=pltpu.VMEM)] * 2,
        compiler_params=pltpu.CompilerParams(vmem_limit_bytes=SUM_BYTES),
        cost_estimate=pl.CostEstimate(flops=0, bytes_accessed=0, transcendentals=0),
    )(bit, mine, came)


def flipped_along(value, axis, bits):
    count = lax.axis_size(axis)
    return lax.ppermute(value, axis, [(source, source ^ bits) for source in range(count)])


def exchanged_sum(parts, bits):
    stages = []
    for level in range(1, len(bits)):
        keep, send = parts
        came = flipped_along(send, "virt", 1 << (level - 1))
        parts = halved(keep, came, bits[level]) if level < len(bits) - 1 else [keep + came]
        stages.append(parts[0])
    total = parts[0]
    return total + flipped_along(total, "virt", 1 << (len(bits) - 1)), stages


def per_device(amplitudes, integrals, occ_pairs, partners, virt_list, eps_occ, eps_virt):
    width = virt_list.shape[0]
    count = lax.axis_size("pair")
    size = lax.axis_size("virt")
    rows = amplitudes.shape[0] // size
    cuts = column_cuts(integrals.shape[1])
    me = lax.axis_index("virt").astype(jnp.int32)
    levels = size.bit_length() - 1
    bits = [((me >> level) & 1).reshape(1) for level in range(levels)]
    order = [sum(((place >> (levels - 1 - level)) & 1) << level for level in range(1, levels)) for place in range(size // 2)]
    upper = me >= size // 2

    def sent(piece):
        return [passed_along(piece, "pair", -shift) for shift in range(1, count)]

    first = integrals[:, cuts[0][0] : cuts[0][1]]
    rest = after(integrals, first)
    pieces = [first] + [rest[:, low:high] for low, high in cuts[1:]]
    in_flight = [sent(pieces[0]), sent(pieces[1])]
    own_product = multiplied(amplitudes, after(rest, pieces), bits[0], order)
    own_sum, own_stages = exchanged_sum(own_product, bits)
    sums = [[own_sum]] + [[] for _ in range(1, count)]
    earlier = own_product
    for step in range(len(cuts)):
        if step > 0:
            earlier = (earlier, (own_stages + [own_sum])[min(step - 1 if step < 3 else len(own_stages), len(own_stages))])
        arrived, earlier = lax.optimization_barrier((in_flight[step], earlier))
        if step + 2 < len(cuts):
            in_flight.append(sent(after(pieces[step + 2], arrived)))
        for shift in range(1, count):
            product = multiplied(amplitudes, arrived[shift - 1], bits[0], order)
            earlier, stages = exchanged_sum(product, bits)
            sums[shift].append(earlier)

    both = in_column_order([jnp.concatenate(parts, axis=1) for parts in sums], count)
    mine = jnp.where(upper, both[rows:], both[:rows])
    other = jnp.where(upper, both[:rows], both[rows:])
    flipped = jnp.take(other, partners % mine.shape[0], axis=0)
    total = mine + transpose_block(flipped, width)

    occ_ids = jnp.arange(eps_occ.shape[0], dtype=jnp.int32)
    occ_match = occ_pairs[:, :, None] == occ_ids[None, None, :]
    occ_sum = jnp.sum(jnp.where(occ_match, eps_occ[None, None, :], 0.0), axis=(1, 2))
    virt_ids = jnp.arange(eps_virt.shape[0], dtype=jnp.int32)
    virt_match = virt_list[:, None] == virt_ids[None, :]
    virt_energy = jnp.sum(jnp.where(virt_match, eps_virt[None, :], 0.0), axis=1)
    virt_sum = (virt_energy[:, None] + virt_energy[None, :]).reshape(-1)
    denominator = virt_sum[None, :] - occ_sum[:, None]
    return total / denominator


def solution(mesh):
    placed = (
        P("pair", "virt"),
        P("virt", "pair"),
        P(("pair", "virt"), None),
        P(("pair", "virt")),
        P(),
        P(),
        P(),
    )
    return jax.shard_map(
        per_device, mesh=mesh, in_specs=placed, out_specs=P(("pair", "virt"), None), check_vma=False
    )
```

```python
import functools

import jax
import jax.numpy as jnp
from jax import lax
from jax.experimental import pallas as pl
from jax.experimental.pallas import tpu as pltpu
from jax.sharding import PartitionSpec as P

DEPTH_CUTS = 4
PRODUCT_BYTES = 51 * 1024 * 1024
SUM_BYTES = 8 * 1024 * 1024


def passed_along(value, axis, steps):
    count = lax.axis_size(axis)
    pairs = [(source, (source + steps) % count) for source in range(count)]
    return lax.ppermute(value, axis, pairs)


def transpose_block(values, width):
    count = values.shape[0]
    return values.reshape(count, width, width).transpose(0, 2, 1).reshape(count, width * width)


def column_cuts(columns):
    half, quarter = columns // 2, columns // 4
    return [(0, half), (half, half + quarter), (half + quarter, columns)]


def after(value, earlier):
    return lax.optimization_barrier((value, earlier))[0]


def in_column_order(blocks, count):
    own = lax.axis_index("pair")
    ordered = []
    for place in range(count):
        block = blocks[place]
        for index in range(1, count):
            block = jnp.where(own == index, blocks[(place - index) % count], block)
        ordered.append(block)
    return jnp.concatenate(ordered, axis=1)


def product_kernel(steps, order, has_base, bit_ref, a_ref, b_ref, *refs):
    base_ref = refs[0] if has_base else None
    keep_ref, send_ref, total_ref = refs[-3:]
    step = pl.program_id(0)
    term = jnp.dot(a_ref[...], b_ref[...], preferred_element_type=jnp.float32)

    @pl.when(step == 0)
    def _():
        total_ref[...] = term + base_ref[...] if has_base else term

    @pl.when(step > 0)
    def _():
        total_ref[...] += term

    @pl.when(step == steps - 1)
    def _():
        rows = keep_ref.shape[0] // len(order)
        for out_ref, bit in ((keep_ref, bit_ref[0]), (send_ref, 1 - bit_ref[0])):
            for place, block in enumerate(order):
                start = pl.multiple_of((block + bit) * rows, rows)
                out_ref[place * rows : (place + 1) * rows, :] = total_ref[pl.ds(start, rows), :]


def multiplied(amplitudes, columns, bit, order, first=0, base=None):
    rows, depth = amplitudes.shape
    width = columns.shape[1]
    part = depth // DEPTH_CUTS
    steps = columns.shape[0] // part
    shape = jax.ShapeDtypeStruct((rows // 2, width), jnp.float32)
    bases = [] if base is None else [base]
    return pl.pallas_call(
        functools.partial(product_kernel, steps, order, base is not None),
        grid=(steps,),
        out_shape=[shape] * 2,
        in_specs=[
            pl.BlockSpec(memory_space=pltpu.SMEM),
            pl.BlockSpec((rows, part), lambda k: (0, k + first)),
            pl.BlockSpec((part, width), lambda k: (k, 0)),
        ]
        + [pl.BlockSpec((rows, width), lambda k: (0, 0)) for _ in bases],
        out_specs=[pl.BlockSpec(shape.shape, lambda k: (0, 0))] * 2,
        scratch_shapes=[pltpu.VMEM((rows, width), jnp.float32)],
        compiler_params=pltpu.CompilerParams(vmem_limit_bytes=PRODUCT_BYTES),
        cost_estimate=pl.CostEstimate(flops=0, bytes_accessed=0, transcendentals=0),
    )(bit, amplitudes, columns, *bases)


def plain_kernel(a_ref, b_ref, out_ref):
    term = jnp.dot(a_ref[...], b_ref[...], preferred_element_type=jnp.float32)

    @pl.when(pl.program_id(0) == 0)
    def _():
        out_ref[...] = term

    @pl.when(pl.program_id(0) > 0)
    def _():
        out_ref[...] += term


def plain_product(amplitudes, columns):
    rows, depth = amplitudes.shape
    width = columns.shape[1]
    part = depth // DEPTH_CUTS
    return pl.pallas_call(
        plain_kernel,
        grid=(columns.shape[0] // part,),
        out_shape=jax.ShapeDtypeStruct((rows, width), jnp.float32),
        in_specs=[
            pl.BlockSpec((rows, part), lambda k: (0, k)),
            pl.BlockSpec((part, width), lambda k: (k, 0)),
        ],
        out_specs=pl.BlockSpec((rows, width), lambda k: (0, 0)),
        compiler_params=pltpu.CompilerParams(vmem_limit_bytes=PRODUCT_BYTES),
        cost_estimate=pl.CostEstimate(flops=0, bytes_accessed=0, transcendentals=0),
    )(amplitudes, columns)


def halve_kernel(bit_ref, mine_ref, came_ref, keep_ref, send_ref):
    rows = keep_ref.shape[0]
    for out_ref, bit in ((keep_ref, bit_ref[0]), (send_ref, 1 - bit_ref[0])):
        part = pl.ds(pl.multiple_of(bit * rows, rows), rows)
        out_ref[...] = mine_ref[part, :] + came_ref[part, :]


def halved(mine, came, bit):
    rows, width = mine.shape
    shape = jax.ShapeDtypeStruct((rows // 2, width), jnp.float32)
    return pl.pallas_call(
        halve_kernel,
        out_shape=[shape] * 2,
        in_specs=[pl.BlockSpec(memory_space=pltpu.SMEM)] + [pl.BlockSpec(memory_space=pltpu.VMEM)] * 2,
        out_specs=[pl.BlockSpec(memory_space=pltpu.VMEM)] * 2,
        compiler_params=pltpu.CompilerParams(vmem_limit_bytes=SUM_BYTES),
        cost_estimate=pl.CostEstimate(flops=0, bytes_accessed=0, transcendentals=0),
    )(bit, mine, came)


def flipped_along(value, axis, bits):
    count = lax.axis_size(axis)
    return lax.ppermute(value, axis, [(source, source ^ bits) for source in range(count)])


def exchanged_sum(parts, bits, gates=()):
    stages = []
    for level in range(1, len(bits)):
        keep, send = parts
        came = flipped_along(send, "virt", 1 << (level - 1))
        if level in gates:
            came = after(came, gates[level])
        parts = halved(keep, came, bits[level]) if level < len(bits) - 1 else [keep + came]
        stages.append(parts[0])
    total = parts[0]
    return total + flipped_along(total, "virt", 1 << (len(bits) - 1)), stages


def per_device(amplitudes, integrals, occ_pairs, partners, virt_list, eps_occ, eps_virt):
    width = virt_list.shape[0]
    count = lax.axis_size("pair")
    size = lax.axis_size("virt")
    rows = amplitudes.shape[0] // size
    cuts = column_cuts(integrals.shape[1])
    me = lax.axis_index("virt").astype(jnp.int32)
    levels = size.bit_length() - 1
    bits = [((me >> level) & 1).reshape(1) for level in range(levels)]
    order = [sum(((place >> (levels - 1 - level)) & 1) << level for level in range(1, levels)) for place in range(size // 2)]
    upper = me >= size // 2

    def sent(piece):
        return [passed_along(piece, "pair", -shift) for shift in range(1, count)]

    first = integrals[:, cuts[0][0] : cuts[0][1]]
    rest = after(integrals, first)
    low, high = cuts[-1]
    late = integrals.shape[0] // DEPTH_CUTS * (DEPTH_CUTS - 1)
    pieces = [first] + [rest[:, low:high] for low, high in cuts[1:-1]] + [rest[:late, low:high], rest[late:, low:high]]
    in_flight = [sent(pieces[0]), sent(pieces[1])]
    own_product = multiplied(amplitudes, after(rest, pieces), bits[0], order)
    own_sum, own_stages = exchanged_sum(own_product, bits)
    sums = [[own_sum]] + [[] for _ in range(1, count)]
    earlier, gates = own_stages[2], {}
    for step in range(len(pieces)):
        if step == 1:
            earlier = (earlier, own_sum)
        arrived, earlier = lax.optimization_barrier((in_flight[step], earlier))
        if step + 2 < len(pieces):
            in_flight.append(sent(after(pieces[step + 2], arrived)))
        if step == len(pieces) - 2:
            bases = [plain_product(amplitudes, columns) for columns in arrived]
            earlier = (gates[2], bases)
            gates = {}
            continue
        for shift in range(1, count):
            if step < len(cuts) - 1:
                product = multiplied(amplitudes, arrived[shift - 1], bits[0], order)
            else:
                product = multiplied(amplitudes, arrived[shift - 1], bits[0], order, DEPTH_CUTS - 1, bases[shift - 1])
            total, stages = exchanged_sum(product, bits, gates)
            sums[shift].append(total)
            earlier, gates = stages[1], {1: stages[2], 2: total}

    both = in_column_order([jnp.concatenate(parts, axis=1) for parts in sums], count)
    mine = jnp.where(upper, both[rows:], both[:rows])
    other = jnp.where(upper, both[:rows], both[rows:])
    flipped = jnp.take(other, partners % mine.shape[0], axis=0)
    total = mine + transpose_block(flipped, width)

    occ_ids = jnp.arange(eps_occ.shape[0], dtype=jnp.int32)
    occ_match = occ_pairs[:, :, None] == occ_ids[None, None, :]
    occ_sum = jnp.sum(jnp.where(occ_match, eps_occ[None, None, :], 0.0), axis=(1, 2))
    virt_ids = jnp.arange(eps_virt.shape[0], dtype=jnp.int32)
    virt_match = virt_list[:, None] == virt_ids[None, :]
    virt_energy = jnp.sum(jnp.where(virt_match, eps_virt[None, :], 0.0), axis=1)
    virt_sum = (virt_energy[:, None] + virt_energy[None, :]).reshape(-1)
    denominator = virt_sum[None, :] - occ_sum[:, None]
    return total / denominator


def solution(mesh):
    placed = (
        P("pair", "virt"),
        P("virt", "pair"),
        P(("pair", "virt"), None),
        P(("pair", "virt")),
        P(),
        P(),
        P(),
    )
    return jax.shard_map(
        per_device, mesh=mesh, in_specs=placed, out_specs=P(("pair", "virt"), None), check_vma=False
    )
```

```python
import functools

import jax
import jax.numpy as jnp
from jax import lax
from jax.experimental import pallas as pl
from jax.experimental.pallas import tpu as pltpu
from jax.sharding import PartitionSpec as P

DEPTH_CUTS = 4
OWN_SPLITS = 2
PRODUCT_BYTES = 51 * 1024 * 1024
SUM_BYTES = 8 * 1024 * 1024


def passed_along(value, axis, steps):
    count = lax.axis_size(axis)
    pairs = [(source, (source + steps) % count) for source in range(count)]
    return lax.ppermute(value, axis, pairs)


def transpose_block(values, width):
    count = values.shape[0]
    return values.reshape(count, width, width).transpose(0, 2, 1).reshape(count, width * width)


def column_cuts(columns):
    half, quarter = columns // 2, columns // 4
    return [(0, half), (half, half + quarter), (half + quarter, columns)]


def after(value, earlier):
    return lax.optimization_barrier((value, earlier))[0]


def in_column_order(blocks, count):
    own = lax.axis_index("pair")
    ordered = []
    for place in range(count):
        block = blocks[place]
        for index in range(1, count):
            block = jnp.where(own == index, blocks[(place - index) % count], block)
        ordered.append(block)
    return jnp.concatenate(ordered, axis=1)


def product_kernel(steps, order, splits, has_base, bit_ref, a_ref, b_ref, *refs):
    base_ref = refs[0] if has_base else None
    out_refs, total_ref = refs[-1 - 2 * splits : -1], refs[-1]
    step = pl.program_id(0)
    term = jnp.dot(a_ref[...], b_ref[...], preferred_element_type=jnp.float32)

    @pl.when(step == 0)
    def _():
        total_ref[...] = term + base_ref[...] if has_base else term

    @pl.when(step > 0)
    def _():
        total_ref[...] += term

    @pl.when(step == steps - 1)
    def _():
        rows, width = out_refs[0].shape
        rows = rows // len(order)
        for index, out_ref in enumerate(out_refs):
            bit = 1 - bit_ref[0] if index % 2 else bit_ref[0]
            columns = slice(index // 2 * width, (index // 2 + 1) * width)
            for place, block in enumerate(order):
                start = pl.multiple_of((block + bit) * rows, rows)
                out_ref[place * rows : (place + 1) * rows, :] = total_ref[pl.ds(start, rows), columns]


def multiplied(amplitudes, columns, bit, order, first=0, base=None, splits=1):
    rows, depth = amplitudes.shape
    width = columns.shape[1]
    part = depth // DEPTH_CUTS
    steps = columns.shape[0] // part
    shape = jax.ShapeDtypeStruct((rows // 2, width // splits), jnp.float32)
    bases = [] if base is None else [base]
    return pl.pallas_call(
        functools.partial(product_kernel, steps, order, splits, base is not None),
        grid=(steps,),
        out_shape=[shape] * (2 * splits),
        in_specs=[
            pl.BlockSpec(memory_space=pltpu.SMEM),
            pl.BlockSpec((rows, part), lambda k: (0, k + first)),
            pl.BlockSpec((part, width), lambda k: (k, 0)),
        ]
        + [pl.BlockSpec((rows, width), lambda k: (0, 0)) for _ in bases],
        out_specs=[pl.BlockSpec(shape.shape, lambda k: (0, 0))] * (2 * splits),
        scratch_shapes=[pltpu.VMEM((rows, width), jnp.float32)],
        compiler_params=pltpu.CompilerParams(vmem_limit_bytes=PRODUCT_BYTES),
        cost_estimate=pl.CostEstimate(flops=0, bytes_accessed=0, transcendentals=0),
    )(bit, amplitudes, columns, *bases)


def plain_kernel(a_ref, b_ref, out_ref):
    term = jnp.dot(a_ref[...], b_ref[...], preferred_element_type=jnp.float32)

    @pl.when(pl.program_id(0) == 0)
    def _():
        out_ref[...] = term

    @pl.when(pl.program_id(0) > 0)
    def _():
        out_ref[...] += term


def plain_product(amplitudes, columns):
    rows, depth = amplitudes.shape
    width = columns.shape[1]
    part = depth // DEPTH_CUTS
    return pl.pallas_call(
        plain_kernel,
        grid=(columns.shape[0] // part,),
        out_shape=jax.ShapeDtypeStruct((rows, width), jnp.float32),
        in_specs=[
            pl.BlockSpec((rows, part), lambda k: (0, k)),
            pl.BlockSpec((part, width), lambda k: (k, 0)),
        ],
        out_specs=pl.BlockSpec((rows, width), lambda k: (0, 0)),
        compiler_params=pltpu.CompilerParams(vmem_limit_bytes=PRODUCT_BYTES),
        cost_estimate=pl.CostEstimate(flops=0, bytes_accessed=0, transcendentals=0),
    )(amplitudes, columns)


def halve_kernel(bit_ref, mine_ref, came_ref, keep_ref, send_ref):
    rows = keep_ref.shape[0]
    for out_ref, bit in ((keep_ref, bit_ref[0]), (send_ref, 1 - bit_ref[0])):
        part = pl.ds(pl.multiple_of(bit * rows, rows), rows)
        out_ref[...] = mine_ref[part, :] + came_ref[part, :]


def halved(mine, came, bit):
    rows, width = mine.shape
    shape = jax.ShapeDtypeStruct((rows // 2, width), jnp.float32)
    return pl.pallas_call(
        halve_kernel,
        out_shape=[shape] * 2,
        in_specs=[pl.BlockSpec(memory_space=pltpu.SMEM)] + [pl.BlockSpec(memory_space=pltpu.VMEM)] * 2,
        out_specs=[pl.BlockSpec(memory_space=pltpu.VMEM)] * 2,
        compiler_params=pltpu.CompilerParams(vmem_limit_bytes=SUM_BYTES),
        cost_estimate=pl.CostEstimate(flops=0, bytes_accessed=0, transcendentals=0),
    )(bit, mine, came)


def flipped_along(value, axis, bits):
    count = lax.axis_size(axis)
    return lax.ppermute(value, axis, [(source, source ^ bits) for source in range(count)])


def exchanged_sum(parts, bits, gates=()):
    stages = []
    for level in range(1, len(bits)):
        keep, send = parts
        came = flipped_along(send, "virt", 1 << (level - 1))
        if level in gates:
            came = after(came, gates[level])
        parts = halved(keep, came, bits[level]) if level < len(bits) - 1 else [keep + came]
        stages.append(parts[0])
    total = parts[0]
    return total + flipped_along(total, "virt", 1 << (len(bits) - 1)), stages


def per_device(amplitudes, integrals, occ_pairs, partners, virt_list, eps_occ, eps_virt):
    width = virt_list.shape[0]
    count = lax.axis_size("pair")
    size = lax.axis_size("virt")
    rows = amplitudes.shape[0] // size
    cuts = column_cuts(integrals.shape[1])
    me = lax.axis_index("virt").astype(jnp.int32)
    levels = size.bit_length() - 1
    bits = [((me >> level) & 1).reshape(1) for level in range(levels)]
    order = [sum(((place >> (levels - 1 - level)) & 1) << level for level in range(1, levels)) for place in range(size // 2)]
    upper = me >= size // 2

    def sent(piece):
        return [passed_along(piece, "pair", -shift) for shift in range(1, count)]

    first = integrals[:, cuts[0][0] : cuts[0][1]]
    rest = after(integrals, first)
    low, high = cuts[-1]
    late = integrals.shape[0] // DEPTH_CUTS * (DEPTH_CUTS - 1)
    pieces = [first] + [rest[:, low:high] for low, high in cuts[1:-1]] + [rest[:late, low:high], rest[late:, low:high]]
    in_flight = [sent(pieces[0]), sent(pieces[1])]
    own_product = multiplied(amplitudes, after(rest, pieces), bits[0], order, splits=OWN_SPLITS)
    own_sums = [exchanged_sum(own_product[2 * part : 2 * part + 2], bits)[0] for part in range(OWN_SPLITS)]
    sums = [own_sums] + [[] for _ in range(1, count)]
    earlier, gates = own_sums, {}
    for step in range(len(pieces)):
        arrived, earlier = lax.optimization_barrier((in_flight[step], earlier))
        if step + 2 < len(pieces):
            in_flight.append(sent(after(pieces[step + 2], arrived)))
        if step == len(pieces) - 2:
            bases = [plain_product(amplitudes, columns) for columns in arrived]
            earlier = (stages[2], bases)
            continue
        for shift in range(1, count):
            if step < len(cuts) - 1:
                product = multiplied(amplitudes, arrived[shift - 1], bits[0], order)
            else:
                product = multiplied(amplitudes, arrived[shift - 1], bits[0], order, DEPTH_CUTS - 1, bases[shift - 1])
            total, stages = exchanged_sum(product, bits, gates)
            sums[shift].append(total)
            earlier, gates = stages[2] if step < len(cuts) - 2 else stages[1], {1: total}

    both = in_column_order([jnp.concatenate(parts, axis=1) for parts in sums], count)
    mine = jnp.where(upper, both[rows:], both[:rows])
    other = jnp.where(upper, both[:rows], both[rows:])
    flipped = jnp.take(other, partners % mine.shape[0], axis=0)
    total = mine + transpose_block(flipped, width)

    occ_ids = jnp.arange(eps_occ.shape[0], dtype=jnp.int32)
    occ_match = occ_pairs[:, :, None] == occ_ids[None, None, :]
    occ_sum = jnp.sum(jnp.where(occ_match, eps_occ[None, None, :], 0.0), axis=(1, 2))
    virt_ids = jnp.arange(eps_virt.shape[0], dtype=jnp.int32)
    virt_match = virt_list[:, None] == virt_ids[None, :]
    virt_energy = jnp.sum(jnp.where(virt_match, eps_virt[None, :], 0.0), axis=1)
    virt_sum = (virt_energy[:, None] + virt_energy[None, :]).reshape(-1)
    denominator = virt_sum[None, :] - occ_sum[:, None]
    return total / denominator


def solution(mesh):
    placed = (
        P("pair", "virt"),
        P("virt", "pair"),
        P(("pair", "virt"), None),
        P(("pair", "virt")),
        P(),
        P(),
        P(),
    )
    return jax.shard_map(
        per_device, mesh=mesh, in_specs=placed, out_specs=P(("pair", "virt"), None), check_vma=False
    )
```

```python
import functools

import jax
import jax.numpy as jnp
from jax import lax
from jax.experimental import pallas as pl
from jax.experimental.pallas import tpu as pltpu
from jax.sharding import PartitionSpec as P

DEPTH_CUTS = 4
ROW_CUTS = 4
FREE = pl.CostEstimate(flops=0, bytes_accessed=0, transcendentals=0)
OWN_SPLITS = 2
PRODUCT_BYTES = 51 * 1024 * 1024
SUM_BYTES = 8 * 1024 * 1024


def passed_along(value, axis, steps):
    count = lax.axis_size(axis)
    pairs = [(source, (source + steps) % count) for source in range(count)]
    return lax.ppermute(value, axis, pairs)


def transpose_block(values, width):
    count = values.shape[0]
    return values.reshape(count, width, width).transpose(0, 2, 1).reshape(count, width * width)


def column_cuts(columns):
    half, quarter = columns // 2, columns // 4
    return [(0, half), (half, half + quarter), (half + quarter, columns)]


def after(value, earlier):
    return lax.optimization_barrier((value, earlier))[0]


def in_column_order(blocks, count):
    own = lax.axis_index("pair")
    ordered = []
    for place in range(count):
        block = blocks[place]
        for index in range(1, count):
            block = jnp.where(own == index, blocks[(place - index) % count], block)
        ordered.append(block)
    return jnp.concatenate(ordered, axis=1)


def add_product(a_refs, b_ref, total_ref, base_ref):
    columns = b_ref[...]
    rows = a_refs[0].shape[0]
    for index, a_ref in enumerate(a_refs):
        part = slice(index * rows, (index + 1) * rows)
        term = jnp.dot(a_ref[...], columns, preferred_element_type=jnp.float32)

        @pl.when(pl.program_id(0) == 0)
        def _():
            total_ref[part, :] = term if base_ref is None else term + base_ref[part, :]

        @pl.when(pl.program_id(0) > 0)
        def _():
            total_ref[part, :] += term


def row_blocks(rows, part, first):
    return [pl.BlockSpec((rows // ROW_CUTS, part), lambda k, j=j: (j, k + first)) for j in range(ROW_CUTS)]


def product_cost(rows, columns):
    depth, width = columns.shape
    return pl.CostEstimate(flops=2 * rows * depth * width, bytes_accessed=2 * rows * depth, transcendentals=0)


def product_kernel(steps, order, splits, has_base, bit_ref, *refs):
    a_refs, b_ref = refs[:ROW_CUTS], refs[ROW_CUTS]
    base_ref = refs[ROW_CUTS + 1] if has_base else None
    out_refs, total_ref = refs[-1 - 2 * splits : -1], refs[-1]
    step = pl.program_id(0)
    add_product(a_refs, b_ref, total_ref, base_ref)

    @pl.when(step == steps - 1)
    def _():
        rows, width = out_refs[0].shape
        rows = rows // len(order)
        for index, out_ref in enumerate(out_refs):
            bit = 1 - bit_ref[0] if index % 2 else bit_ref[0]
            columns = slice(index // 2 * width, (index // 2 + 1) * width)
            for place, block in enumerate(order):
                start = pl.multiple_of((block + bit) * rows, rows)
                out_ref[place * rows : (place + 1) * rows, :] = total_ref[pl.ds(start, rows), columns]


def multiplied(amplitudes, columns, bit, order, first=0, base=None, splits=1):
    rows, depth = amplitudes.shape
    width = columns.shape[1]
    part = depth // DEPTH_CUTS
    steps = columns.shape[0] // part
    shape = jax.ShapeDtypeStruct((rows // 2, width // splits), jnp.float32)
    bases = [] if base is None else [base]
    return pl.pallas_call(
        functools.partial(product_kernel, steps, order, splits, base is not None),
        grid=(steps,),
        out_shape=[shape] * (2 * splits),
        in_specs=[
            pl.BlockSpec(memory_space=pltpu.SMEM),
            *row_blocks(rows, part, first),
            pl.BlockSpec((part, width), lambda k: (k, 0)),
        ]
        + [pl.BlockSpec((rows, width), lambda k: (0, 0)) for _ in bases],
        out_specs=[pl.BlockSpec(shape.shape, lambda k: (0, 0))] * (2 * splits),
        scratch_shapes=[pltpu.VMEM((rows, width), jnp.float32)],
        compiler_params=pltpu.CompilerParams(vmem_limit_bytes=PRODUCT_BYTES),
        cost_estimate=product_cost(rows, columns) if splits == 1 else FREE,
    )(bit, *[amplitudes] * ROW_CUTS, columns, *bases)


def plain_kernel(*refs):
    add_product(refs[:ROW_CUTS], refs[ROW_CUTS], refs[-1], None)


def plain_product(amplitudes, columns):
    rows, depth = amplitudes.shape
    width = columns.shape[1]
    part = depth // DEPTH_CUTS
    return pl.pallas_call(
        plain_kernel,
        grid=(columns.shape[0] // part,),
        out_shape=jax.ShapeDtypeStruct((rows, width), jnp.float32),
        in_specs=[
            *row_blocks(rows, part, 0),
            pl.BlockSpec((part, width), lambda k: (k, 0)),
        ],
        out_specs=pl.BlockSpec((rows, width), lambda k: (0, 0)),
        compiler_params=pltpu.CompilerParams(vmem_limit_bytes=PRODUCT_BYTES),
        cost_estimate=product_cost(rows, columns),
    )(*[amplitudes] * ROW_CUTS, columns)


def halve_kernel(bit_ref, mine_ref, came_ref, keep_ref, send_ref):
    rows = keep_ref.shape[0]
    for out_ref, bit in ((keep_ref, bit_ref[0]), (send_ref, 1 - bit_ref[0])):
        part = pl.ds(pl.multiple_of(bit * rows, rows), rows)
        out_ref[...] = mine_ref[part, :] + came_ref[part, :]


def halved(mine, came, bit):
    rows, width = mine.shape
    shape = jax.ShapeDtypeStruct((rows // 2, width), jnp.float32)
    return pl.pallas_call(
        halve_kernel,
        out_shape=[shape] * 2,
        in_specs=[pl.BlockSpec(memory_space=pltpu.SMEM)] + [pl.BlockSpec(memory_space=pltpu.VMEM)] * 2,
        out_specs=[pl.BlockSpec(memory_space=pltpu.VMEM)] * 2,
        compiler_params=pltpu.CompilerParams(vmem_limit_bytes=SUM_BYTES),
        cost_estimate=FREE,
    )(bit, mine, came)


def flipped_along(value, axis, bits):
    count = lax.axis_size(axis)
    return lax.ppermute(value, axis, [(source, source ^ bits) for source in range(count)])


def exchanged_sum(parts, bits, gates=()):
    stages = []
    for level in range(1, len(bits)):
        keep, send = parts
        came = flipped_along(send, "virt", 1 << (level - 1))
        if level in gates:
            came = after(came, gates[level])
        parts = halved(keep, came, bits[level]) if level < len(bits) - 1 else [keep + came]
        stages.append(parts[0])
    total = parts[0]
    return total + flipped_along(total, "virt", 1 << (len(bits) - 1)), stages


def per_device(amplitudes, integrals, occ_pairs, partners, virt_list, eps_occ, eps_virt):
    width = virt_list.shape[0]
    count = lax.axis_size("pair")
    size = lax.axis_size("virt")
    rows = amplitudes.shape[0] // size
    cuts = column_cuts(integrals.shape[1])
    me = lax.axis_index("virt").astype(jnp.int32)
    levels = size.bit_length() - 1
    bits = [((me >> level) & 1).reshape(1) for level in range(levels)]
    order = [sum(((place >> (levels - 1 - level)) & 1) << level for level in range(1, levels)) for place in range(size // 2)]
    upper = me >= size // 2

    def sent(piece):
        return [passed_along(piece, "pair", -shift) for shift in range(1, count)]

    first = integrals[:, cuts[0][0] : cuts[0][1]]
    rest = after(integrals, first)
    low, high = cuts[-1]
    late = integrals.shape[0] // DEPTH_CUTS * (DEPTH_CUTS - 1)
    pieces = [first] + [rest[:, low:high] for low, high in cuts[1:-1]] + [rest[:late, low:high], rest[late:, low:high]]
    in_flight = [sent(pieces[0]), sent(pieces[1])]
    own_product = multiplied(amplitudes, after(rest, pieces), bits[0], order, splits=OWN_SPLITS)
    own_sums = [exchanged_sum(own_product[2 * part : 2 * part + 2], bits)[0] for part in range(OWN_SPLITS)]
    sums = [own_sums] + [[] for _ in range(1, count)]
    in_flight += [sent(after(piece, own_sums)) for piece in pieces[2:]]
    earlier, gates = own_sums, {}
    for step in range(len(pieces)):
        arrived, earlier = lax.optimization_barrier((in_flight[step], earlier))
        if step == len(pieces) - 2:
            bases = [plain_product(amplitudes, columns) for columns in arrived]
            earlier = (stages[2], bases)
            continue
        for shift in range(1, count):
            if step < len(cuts) - 1:
                product = multiplied(amplitudes, arrived[shift - 1], bits[0], order)
            else:
                product = multiplied(amplitudes, arrived[shift - 1], bits[0], order, DEPTH_CUTS - 1, bases[shift - 1])
            total, stages = exchanged_sum(product, bits, gates)
            sums[shift].append(total)
            earlier, gates = stages[2] if step < len(cuts) - 2 else stages[0], {2: total}

    both = in_column_order([jnp.concatenate(parts, axis=1) for parts in sums], count)
    mine = jnp.where(upper, both[rows:], both[:rows])
    other = jnp.where(upper, both[:rows], both[rows:])
    flipped = jnp.take(other, partners % mine.shape[0], axis=0)
    total = mine + transpose_block(flipped, width)

    occ_ids = jnp.arange(eps_occ.shape[0], dtype=jnp.int32)
    occ_match = occ_pairs[:, :, None] == occ_ids[None, None, :]
    occ_sum = jnp.sum(jnp.where(occ_match, eps_occ[None, None, :], 0.0), axis=(1, 2))
    virt_ids = jnp.arange(eps_virt.shape[0], dtype=jnp.int32)
    virt_match = virt_list[:, None] == virt_ids[None, :]
    virt_energy = jnp.sum(jnp.where(virt_match, eps_virt[None, :], 0.0), axis=1)
    virt_sum = (virt_energy[:, None] + virt_energy[None, :]).reshape(-1)
    denominator = virt_sum[None, :] - occ_sum[:, None]
    return total / denominator


def solution(mesh):
    placed = (
        P("pair", "virt"),
        P("virt", "pair"),
        P(("pair", "virt"), None),
        P(("pair", "virt")),
        P(),
        P(),
        P(),
    )
    return jax.shard_map(
        per_device, mesh=mesh, in_specs=placed, out_specs=P(("pair", "virt"), None), check_vma=False
    )
```

```python
import functools

import jax
import jax.numpy as jnp
from jax import lax
from jax.experimental import pallas as pl
from jax.experimental.pallas import tpu as pltpu
from jax.sharding import PartitionSpec as P

LANES = 128
DEPTH_CUTS = 4
ROW_CUTS = 1
FREE = pl.CostEstimate(flops=0, bytes_accessed=0, transcendentals=0)
OWN_SPLITS = 2
PRODUCT_BYTES = 51 * 1024 * 1024
SUM_BYTES = 8 * 1024 * 1024


def passed_along(value, axis, steps):
    count = lax.axis_size(axis)
    pairs = [(source, (source + steps) % count) for source in range(count)]
    return lax.ppermute(value, axis, pairs)


def transpose_block(values, width):
    count = values.shape[0]
    return values.reshape(count, width, width).transpose(0, 2, 1).reshape(count, width * width)


def column_cuts(columns):
    half, quarter = columns // 2, columns // 4
    return [(0, half), (half, half + quarter), (half + quarter, columns)]


def after(value, earlier):
    return lax.optimization_barrier((value, earlier))[0]


def in_column_order(blocks, count):
    own = lax.axis_index("pair")
    ordered = []
    for place in range(count):
        block = blocks[place]
        for index in range(1, count):
            block = jnp.where(own == index, blocks[(place - index) % count], block)
        ordered.append(block)
    return jnp.concatenate(ordered, axis=1)


def add_product(a_refs, b_ref, total_ref, base_ref):
    columns = b_ref[...]
    rows = a_refs[0].shape[0]
    for index, a_ref in enumerate(a_refs):
        part = slice(index * rows, (index + 1) * rows)
        term = jnp.dot(a_ref[...], columns, preferred_element_type=jnp.float32)

        @pl.when(pl.program_id(0) == 0)
        def _():
            total_ref[part, :] = term if base_ref is None else term + base_ref[part, :]

        @pl.when(pl.program_id(0) > 0)
        def _():
            total_ref[part, :] += term


def row_blocks(rows, part, first):
    return [pl.BlockSpec((rows // ROW_CUTS, part), lambda k, j=j: (j, k + first)) for j in range(ROW_CUTS)]


def product_cost(rows, columns):
    depth, width = columns.shape
    return pl.CostEstimate(flops=2 * rows * depth * width, bytes_accessed=2 * rows * depth, transcendentals=0)


def product_kernel(steps, order, splits, has_base, bit_ref, *refs):
    a_refs, b_ref = refs[:ROW_CUTS], refs[ROW_CUTS]
    base_ref = refs[ROW_CUTS + 1] if has_base else None
    out_refs, total_ref = refs[-1 - 2 * splits : -1], refs[-1]
    step = pl.program_id(0)
    add_product(a_refs, b_ref, total_ref, base_ref)

    @pl.when(step == steps - 1)
    def _():
        rows, width = out_refs[0].shape
        rows = rows // len(order)
        for index, out_ref in enumerate(out_refs):
            bit = 1 - bit_ref[0] if index % 2 else bit_ref[0]
            columns = slice(index // 2 * width, (index // 2 + 1) * width)
            for place, block in enumerate(order):
                start = pl.multiple_of((block + bit) * rows, rows)
                out_ref[place * rows : (place + 1) * rows, :] = total_ref[pl.ds(start, rows), columns]


def multiplied(amplitudes, columns, bit, order, first=0, base=None, splits=1):
    rows, depth = amplitudes.shape
    width = columns.shape[1]
    part = depth // DEPTH_CUTS
    steps = columns.shape[0] // part
    shape = jax.ShapeDtypeStruct((rows // 2, width // splits), jnp.float32)
    bases = [] if base is None else [base]
    return pl.pallas_call(
        functools.partial(product_kernel, steps, order, splits, base is not None),
        grid=(steps,),
        out_shape=[shape] * (2 * splits),
        in_specs=[
            pl.BlockSpec(memory_space=pltpu.SMEM),
            *row_blocks(rows, part, first),
            pl.BlockSpec((part, width), lambda k: (k, 0)),
        ]
        + [pl.BlockSpec((rows, width), lambda k: (0, 0)) for _ in bases],
        out_specs=[pl.BlockSpec(shape.shape, lambda k: (0, 0))] * (2 * splits),
        scratch_shapes=[pltpu.VMEM((rows, width), jnp.float32)],
        compiler_params=pltpu.CompilerParams(vmem_limit_bytes=PRODUCT_BYTES),
        cost_estimate=product_cost(rows, columns) if splits == 1 else FREE,
    )(bit, *[amplitudes] * ROW_CUTS, columns, *bases)


def plain_kernel(*refs):
    add_product(refs[:ROW_CUTS], refs[ROW_CUTS], refs[-1], None)


def plain_product(amplitudes, columns):
    rows, depth = amplitudes.shape
    width = columns.shape[1]
    part = depth // DEPTH_CUTS
    return pl.pallas_call(
        plain_kernel,
        grid=(columns.shape[0] // part,),
        out_shape=jax.ShapeDtypeStruct((rows, width), jnp.float32),
        in_specs=[
            *row_blocks(rows, part, 0),
            pl.BlockSpec((part, width), lambda k: (k, 0)),
        ],
        out_specs=pl.BlockSpec((rows, width), lambda k: (0, 0)),
        compiler_params=pltpu.CompilerParams(vmem_limit_bytes=PRODUCT_BYTES),
        cost_estimate=product_cost(rows, columns),
    )(*[amplitudes] * ROW_CUTS, columns)


def halve_kernel(bit_ref, mine_ref, came_ref, keep_ref, send_ref):
    rows = keep_ref.shape[0]
    for out_ref, bit in ((keep_ref, bit_ref[0]), (send_ref, 1 - bit_ref[0])):
        part = pl.ds(pl.multiple_of(bit * rows, rows), rows)
        out_ref[...] = mine_ref[part, :] + came_ref[part, :]


def halved(mine, came, bit):
    rows, width = mine.shape
    shape = jax.ShapeDtypeStruct((rows // 2, width), jnp.float32)
    return pl.pallas_call(
        halve_kernel,
        out_shape=[shape] * 2,
        in_specs=[pl.BlockSpec(memory_space=pltpu.SMEM)] + [pl.BlockSpec(memory_space=pltpu.VMEM)] * 2,
        out_specs=[pl.BlockSpec(memory_space=pltpu.VMEM)] * 2,
        compiler_params=pltpu.CompilerParams(vmem_limit_bytes=SUM_BYTES),
        cost_estimate=FREE,
    )(bit, mine, came)


def flipped_along(value, axis, bits):
    count = lax.axis_size(axis)
    return lax.ppermute(value, axis, [(source, source ^ bits) for source in range(count)])


def exchanged_sum(parts, bits, gates=()):
    stages = []
    for level in range(1, len(bits)):
        keep, send = parts
        came = flipped_along(send, "virt", 1 << (level - 1))
        if level in gates:
            came = after(came, gates[level])
        parts = halved(keep, came, bits[level]) if level < len(bits) - 1 else [keep + came]
        stages.append(parts[0])
    total = parts[0]
    return total + flipped_along(total, "virt", 1 << (len(bits) - 1)), stages


def cut_kernel(boxes, source_ref, *refs):
    copies = []
    for index, (rows, columns) in enumerate(boxes):
        part = (rows[1] - rows[0]) // DEPTH_CUTS
        for low in range(0, rows[1] - rows[0], part):
            source = source_ref.at[rows[0] + low : rows[0] + low + part, columns[0] : columns[1]]
            target = refs[index].at[low : low + part, :]
            copies.append(pltpu.make_async_copy(source, target, refs[-1].at[len(copies)]))
    for copy in copies:
        copy.start()
    for copy in copies:
        copy.wait()


def cut_out(source, boxes):
    if any(edge % LANES for _, columns in boxes for edge in columns):
        return [source[rows[0] : rows[1], columns[0] : columns[1]] for rows, columns in boxes]
    anywhere = pl.BlockSpec(memory_space=pl.ANY)
    return pl.pallas_call(
        functools.partial(cut_kernel, boxes),
        out_shape=[jax.ShapeDtypeStruct((r[1] - r[0], c[1] - c[0]), source.dtype) for r, c in boxes],
        in_specs=[anywhere],
        out_specs=[anywhere] * len(boxes),
        scratch_shapes=[pltpu.SemaphoreType.DMA((len(boxes) * DEPTH_CUTS,))],
        cost_estimate=FREE,
    )(source)


def per_device(amplitudes, integrals, occ_pairs, partners, virt_list, eps_occ, eps_virt):
    width = virt_list.shape[0]
    count = lax.axis_size("pair")
    size = lax.axis_size("virt")
    rows = amplitudes.shape[0] // size
    cuts = column_cuts(integrals.shape[1])
    me = lax.axis_index("virt").astype(jnp.int32)
    levels = size.bit_length() - 1
    bits = [((me >> level) & 1).reshape(1) for level in range(levels)]
    order = [sum(((place >> (levels - 1 - level)) & 1) << level for level in range(1, levels)) for place in range(size // 2)]
    upper = me >= size // 2

    def sent(piece):
        return [passed_along(piece, "pair", -shift) for shift in range(1, count)]

    depth = integrals.shape[0]
    late = depth // DEPTH_CUTS * (DEPTH_CUTS - 1)
    first = cut_out(integrals, [((0, depth), cuts[0])])[0]
    rest = after(integrals, first)
    pieces = [first, *cut_out(rest, [((0, depth), cut) for cut in cuts[1:-1]] + [((0, late), cuts[-1]), ((late, depth), cuts[-1])])]
    in_flight = [sent(pieces[0]), sent(pieces[1])]
    own_product = multiplied(amplitudes, after(rest, pieces), bits[0], order, splits=OWN_SPLITS)
    own_sums = [exchanged_sum(own_product[2 * part : 2 * part + 2], bits)[0] for part in range(OWN_SPLITS)]
    sums = [own_sums] + [[] for _ in range(1, count)]
    in_flight += [sent(after(piece, own_sums)) for piece in pieces[2:]]
    earlier, gates = own_sums, {}
    for step in range(len(pieces)):
        arrived, earlier = lax.optimization_barrier((in_flight[step], earlier))
        if step == len(pieces) - 2:
            bases = [plain_product(amplitudes, columns) for columns in arrived]
            earlier = (stages[2], bases)
            continue
        for shift in range(1, count):
            if step < len(cuts) - 1:
                product = multiplied(amplitudes, arrived[shift - 1], bits[0], order)
            else:
                product = multiplied(amplitudes, arrived[shift - 1], bits[0], order, DEPTH_CUTS - 1, bases[shift - 1])
            total, stages = exchanged_sum(product, bits, gates)
            sums[shift].append(total)
            earlier, gates = stages[2] if step < len(cuts) - 2 else stages[0], {2: total}

    both = in_column_order([jnp.concatenate(parts, axis=1) for parts in sums], count)
    mine = jnp.where(upper, both[rows:], both[:rows])
    other = jnp.where(upper, both[:rows], both[rows:])
    flipped = jnp.take(other, partners % mine.shape[0], axis=0)
    total = mine + transpose_block(flipped, width)

    occ_ids = jnp.arange(eps_occ.shape[0], dtype=jnp.int32)
    occ_match = occ_pairs[:, :, None] == occ_ids[None, None, :]
    occ_sum = jnp.sum(jnp.where(occ_match, eps_occ[None, None, :], 0.0), axis=(1, 2))
    virt_ids = jnp.arange(eps_virt.shape[0], dtype=jnp.int32)
    virt_match = virt_list[:, None] == virt_ids[None, :]
    virt_energy = jnp.sum(jnp.where(virt_match, eps_virt[None, :], 0.0), axis=1)
    virt_sum = (virt_energy[:, None] + virt_energy[None, :]).reshape(-1)
    denominator = virt_sum[None, :] - occ_sum[:, None]
    return total / denominator


def solution(mesh):
    placed = (
        P("pair", "virt"),
        P("virt", "pair"),
        P(("pair", "virt"), None),
        P(("pair", "virt")),
        P(),
        P(),
        P(),
    )
    return jax.shard_map(
        per_device, mesh=mesh, in_specs=placed, out_specs=P(("pair", "virt"), None), check_vma=False
    )
```

```python
import functools

import jax
import jax.numpy as jnp
from jax import lax
from jax.experimental import pallas as pl
from jax.experimental.pallas import tpu as pltpu
from jax.sharding import PartitionSpec as P

LANES = 128
DEPTH_CUTS = 4
ROW_CUTS = 1
FREE = pl.CostEstimate(flops=0, bytes_accessed=0, transcendentals=0)
OWN_SPLITS = 2
PRODUCT_BYTES = 51 * 1024 * 1024
CUT_BYTES = 56 * 1024 * 1024
SUM_BYTES = 8 * 1024 * 1024


def passed_along(value, axis, steps):
    count = lax.axis_size(axis)
    pairs = [(source, (source + steps) % count) for source in range(count)]
    return lax.ppermute(value, axis, pairs)


def transpose_block(values, width):
    count = values.shape[0]
    return values.reshape(count, width, width).transpose(0, 2, 1).reshape(count, width * width)


def column_cuts(columns):
    half, quarter = columns // 2, columns // 4
    return [(0, half), (half, half + quarter), (half + quarter, columns)]


def after(value, earlier):
    return lax.optimization_barrier((value, earlier))[0]


def in_column_order(blocks, count):
    own = lax.axis_index("pair")
    ordered = []
    for place in range(count):
        block = blocks[place]
        for index in range(1, count):
            block = jnp.where(own == index, blocks[(place - index) % count], block)
        ordered.append(block)
    return jnp.concatenate(ordered, axis=1)


def add_product(a_refs, b_ref, total_ref, base_ref):
    columns = b_ref[...]
    rows = a_refs[0].shape[0]
    for index, a_ref in enumerate(a_refs):
        part = slice(index * rows, (index + 1) * rows)
        term = jnp.dot(a_ref[...], columns, preferred_element_type=jnp.float32)

        @pl.when(pl.program_id(0) == 0)
        def _():
            total_ref[part, :] = term if base_ref is None else term + base_ref[part, :]

        @pl.when(pl.program_id(0) > 0)
        def _():
            total_ref[part, :] += term


def row_blocks(rows, part, first):
    return [pl.BlockSpec((rows // ROW_CUTS, part), lambda k, j=j: (j, k + first)) for j in range(ROW_CUTS)]


def product_cost(rows, columns):
    depth, width = columns.shape
    return pl.CostEstimate(flops=2 * rows * depth * width, bytes_accessed=2 * rows * depth, transcendentals=0)


def product_kernel(steps, order, splits, has_base, bit_ref, *refs):
    a_refs, b_ref = refs[:ROW_CUTS], refs[ROW_CUTS]
    base_ref = refs[ROW_CUTS + 1] if has_base else None
    out_refs, total_ref = refs[-1 - 2 * splits : -1], refs[-1]
    step = pl.program_id(0)
    add_product(a_refs, b_ref, total_ref, base_ref)

    @pl.when(step == steps - 1)
    def _():
        rows, width = out_refs[0].shape
        rows = rows // len(order)
        for index, out_ref in enumerate(out_refs):
            bit = 1 - bit_ref[0] if index % 2 else bit_ref[0]
            columns = slice(index // 2 * width, (index // 2 + 1) * width)
            for place, block in enumerate(order):
                start = pl.multiple_of((block + bit) * rows, rows)
                out_ref[place * rows : (place + 1) * rows, :] = total_ref[pl.ds(start, rows), columns]


def multiplied(amplitudes, columns, bit, order, first=0, base=None, splits=1):
    rows, depth = amplitudes.shape
    width = columns.shape[1]
    part = depth // DEPTH_CUTS
    steps = columns.shape[0] // part
    shape = jax.ShapeDtypeStruct((rows // 2, width // splits), jnp.float32)
    bases = [] if base is None else [base]
    return pl.pallas_call(
        functools.partial(product_kernel, steps, order, splits, base is not None),
        grid=(steps,),
        out_shape=[shape] * (2 * splits),
        in_specs=[
            pl.BlockSpec(memory_space=pltpu.SMEM),
            *row_blocks(rows, part, first),
            pl.BlockSpec((part, width), lambda k: (k, 0)),
        ]
        + [pl.BlockSpec((rows, width), lambda k: (0, 0)) for _ in bases],
        out_specs=[pl.BlockSpec(shape.shape, lambda k: (0, 0))] * (2 * splits),
        scratch_shapes=[pltpu.VMEM((rows, width), jnp.float32)],
        compiler_params=pltpu.CompilerParams(vmem_limit_bytes=PRODUCT_BYTES),
        cost_estimate=product_cost(rows, columns) if splits == 1 else FREE,
    )(bit, *[amplitudes] * ROW_CUTS, columns, *bases)


def plain_kernel(*refs):
    add_product(refs[:ROW_CUTS], refs[ROW_CUTS], refs[-1], None)


def plain_product(amplitudes, columns):
    rows, depth = amplitudes.shape
    width = columns.shape[1]
    part = depth // DEPTH_CUTS
    return pl.pallas_call(
        plain_kernel,
        grid=(columns.shape[0] // part,),
        out_shape=jax.ShapeDtypeStruct((rows, width), jnp.float32),
        in_specs=[
            *row_blocks(rows, part, 0),
            pl.BlockSpec((part, width), lambda k: (k, 0)),
        ],
        out_specs=pl.BlockSpec((rows, width), lambda k: (0, 0)),
        compiler_params=pltpu.CompilerParams(vmem_limit_bytes=PRODUCT_BYTES),
        cost_estimate=product_cost(rows, columns),
    )(*[amplitudes] * ROW_CUTS, columns)


def halve_kernel(bit_ref, mine_ref, came_ref, keep_ref, send_ref):
    rows = keep_ref.shape[0]
    for out_ref, bit in ((keep_ref, bit_ref[0]), (send_ref, 1 - bit_ref[0])):
        part = pl.ds(pl.multiple_of(bit * rows, rows), rows)
        out_ref[...] = mine_ref[part, :] + came_ref[part, :]


def halved(mine, came, bit):
    rows, width = mine.shape
    shape = jax.ShapeDtypeStruct((rows // 2, width), jnp.float32)
    return pl.pallas_call(
        halve_kernel,
        out_shape=[shape] * 2,
        in_specs=[pl.BlockSpec(memory_space=pltpu.SMEM)] + [pl.BlockSpec(memory_space=pltpu.VMEM)] * 2,
        out_specs=[pl.BlockSpec(memory_space=pltpu.VMEM)] * 2,
        compiler_params=pltpu.CompilerParams(vmem_limit_bytes=SUM_BYTES),
        cost_estimate=FREE,
    )(bit, mine, came)


def flipped_along(value, axis, bits):
    count = lax.axis_size(axis)
    return lax.ppermute(value, axis, [(source, source ^ bits) for source in range(count)])


def exchanged_sum(parts, bits, gates=()):
    stages = []
    for level in range(1, len(bits)):
        keep, send = parts
        came = flipped_along(send, "virt", 1 << (level - 1))
        if level in gates:
            came = after(came, gates[level])
        parts = halved(keep, came, bits[level]) if level < len(bits) - 1 else [keep + came]
        stages.append(parts[0])
    return (parts[0], flipped_along(parts[0], "virt", 1 << (len(bits) - 1))), stages


WHOLE = pl.BlockSpec(memory_space=pltpu.VMEM)


def cut_kernel(boxes, source_ref, *refs):
    copies = []
    for index, (rows, columns) in enumerate(boxes):
        part = (rows[1] - rows[0]) // DEPTH_CUTS
        for low in range(0, rows[1] - rows[0], part):
            source = source_ref.at[rows[0] + low : rows[0] + low + part, columns[0] : columns[1]]
            target = refs[index].at[low : low + part, :]
            copies.append(pltpu.make_async_copy(source, target, refs[-1].at[len(copies)]))
    for copy in copies:
        copy.start()
    for copy in copies:
        copy.wait()


def cut_out(source, rows, columns):
    if columns[0] % LANES or columns[1] % LANES:
        return source[rows[0] : rows[1], columns[0] : columns[1]]
    return pl.pallas_call(
        functools.partial(cut_kernel, [(rows, columns)]),
        out_shape=[jax.ShapeDtypeStruct((rows[1] - rows[0], columns[1] - columns[0]), source.dtype)],
        in_specs=[pl.BlockSpec(memory_space=pl.ANY)],
        out_specs=[WHOLE],
        scratch_shapes=[pltpu.SemaphoreType.DMA((DEPTH_CUTS,))],
        compiler_params=pltpu.CompilerParams(vmem_limit_bytes=CUT_BYTES),
        cost_estimate=FREE,
    )(source)[0]


def last_kernel(width, starts, where_ref, rows_ref, virt_ref, occ_ref, *refs):
    blocks, (out_ref, both_ref, tall_ref, turned_ref) = refs[:-4], refs[-4:]
    rows = out_ref.shape[0]
    for index, start in enumerate(starts):
        value = blocks[index][...]
        if index == len(starts) - 1:
            value = value + blocks[index + 1][...]
        columns = out_ref.shape[1] // 2
        side = where_ref[1] if start < columns else 1 - where_ref[1]
        place = pl.multiple_of(side * columns + start % columns, LANES)
        both_ref[:, pl.ds(place, value.shape[1])] = value
    upper = where_ref[0]
    mine = both_ref[pl.ds(pl.multiple_of(upper * rows, rows), rows), :]
    other = both_ref[pl.ds(pl.multiple_of((1 - upper) * rows, rows), rows), :]
    chosen = (rows_ref[...] == lax.broadcasted_iota(jnp.int32, (rows, rows), 1)).astype(jnp.float32)
    flipped = jnp.dot(chosen, other, precision=lax.Precision.HIGHEST, preferred_element_type=jnp.float32)
    tall_ref[...] = flipped.T
    for b in range(width):
        turned_ref[b * width : (b + 1) * width, :] = tall_ref[pl.ds(b, width, stride=width), :]
    out_ref[...] = (mine + turned_ref[...].T) / (virt_ref[...] - occ_ref[...])


def last_steps(blocks, where, local_rows, virt_sum, occ_sum, width):
    rows = occ_sum.shape[0]
    columns = virt_sum.shape[0]
    starts, start = [], 0
    for block in blocks[:-1]:
        starts.append(start)
        start += block.shape[1]
    return pl.pallas_call(
        functools.partial(last_kernel, width, starts),
        out_shape=jax.ShapeDtypeStruct((rows, columns), jnp.float32),
        in_specs=[pl.BlockSpec(memory_space=pltpu.SMEM)] + [WHOLE] * (3 + len(blocks)),
        out_specs=WHOLE,
        scratch_shapes=[
            pltpu.VMEM((2 * rows, columns), jnp.float32),
            pltpu.VMEM((columns, rows), jnp.float32),
            pltpu.VMEM((columns, rows), jnp.float32),
        ],
        compiler_params=pltpu.CompilerParams(vmem_limit_bytes=SUM_BYTES),
        cost_estimate=FREE,
    )(where, local_rows.reshape(rows, 1), virt_sum.reshape(1, columns), occ_sum.reshape(rows, 1), *blocks)


def per_device(amplitudes, integrals, occ_pairs, partners, virt_list, eps_occ, eps_virt):
    width = virt_list.shape[0]
    count = lax.axis_size("pair")
    size = lax.axis_size("virt")
    rows = amplitudes.shape[0] // size
    cuts = column_cuts(integrals.shape[1])
    me = lax.axis_index("virt").astype(jnp.int32)
    levels = size.bit_length() - 1
    bits = [((me >> level) & 1).reshape(1) for level in range(levels)]
    order = [sum(((place >> (levels - 1 - level)) & 1) << level for level in range(1, levels)) for place in range(size // 2)]
    upper = me >= size // 2

    def sent(piece):
        return [passed_along(piece, "pair", -shift) for shift in range(1, count)]

    depth = integrals.shape[0]
    late = depth // DEPTH_CUTS * (DEPTH_CUTS - 1)
    first = cut_out(integrals, (0, depth), cuts[0])
    rest = after(integrals, first)
    low, high = cuts[-1]
    pieces = [first] + [rest[:, low:high] for low, high in cuts[1:-1]] + [rest[:late, low:high], rest[late:, low:high]]
    in_flight = [sent(pieces[0]), sent(pieces[1])]
    own_product = multiplied(amplitudes, after(rest, pieces), bits[0], order, splits=OWN_SPLITS)
    own_sums = [jnp.add(*exchanged_sum(own_product[2 * part : 2 * part + 2], bits)[0]) for part in range(OWN_SPLITS)]
    sums = [own_sums] + [[] for _ in range(1, count)]
    in_flight += [sent(after(piece, own_sums)) for piece in pieces[2:]]
    earlier, gates = own_sums, {}
    for step in range(len(pieces)):
        arrived, earlier = lax.optimization_barrier((in_flight[step], earlier))
        if step == len(pieces) - 2:
            bases = [plain_product(amplitudes, columns) for columns in arrived]
            earlier = (stages[2], bases)
            continue
        for shift in range(1, count):
            if step < len(cuts) - 1:
                product = multiplied(amplitudes, arrived[shift - 1], bits[0], order)
            else:
                product = multiplied(amplitudes, arrived[shift - 1], bits[0], order, DEPTH_CUTS - 1, bases[shift - 1])
            terms, stages = exchanged_sum(product, bits, gates)
            total = jnp.add(*terms)
            sums[shift].append(total)
            earlier, gates = stages[2] if step < len(cuts) - 2 else stages[0], {2: total}

    occ_ids = jnp.arange(eps_occ.shape[0], dtype=jnp.int32)
    occ_match = occ_pairs[:, :, None] == occ_ids[None, None, :]
    occ_sum = jnp.sum(jnp.where(occ_match, eps_occ[None, None, :], 0.0), axis=(1, 2))
    virt_ids = jnp.arange(eps_virt.shape[0], dtype=jnp.int32)
    virt_match = virt_list[:, None] == virt_ids[None, :]
    virt_energy = jnp.sum(jnp.where(virt_match, eps_virt[None, :], 0.0), axis=1)
    virt_sum = (virt_energy[:, None] + virt_energy[None, :]).reshape(-1)
    if count == 2 and all(block.shape[1] % LANES == 0 for parts in sums for block in parts):
        where = jnp.stack([upper.astype(jnp.int32), lax.axis_index("pair").astype(jnp.int32)])
        blocks = [*sums[0], *sums[1][:-1], *terms]
        return last_steps(blocks, where, partners % rows, virt_sum, occ_sum, width)
    both = in_column_order([jnp.concatenate(parts, axis=1) for parts in sums], count)
    mine = jnp.where(upper, both[rows:], both[:rows])
    other = jnp.where(upper, both[:rows], both[rows:])
    flipped = jnp.take(other, partners % mine.shape[0], axis=0)
    total = mine + transpose_block(flipped, width)

    denominator = virt_sum[None, :] - occ_sum[:, None]
    return total / denominator


def solution(mesh):
    placed = (
        P("pair", "virt"),
        P("virt", "pair"),
        P(("pair", "virt"), None),
        P(("pair", "virt")),
        P(),
        P(),
        P(),
    )
    return jax.shard_map(
        per_device, mesh=mesh, in_specs=placed, out_specs=P(("pair", "virt"), None), check_vma=False
    )
```

```python
import functools

import jax
import jax.numpy as jnp
from jax import lax
from jax.experimental import pallas as pl
from jax.experimental.pallas import tpu as pltpu
from jax.sharding import PartitionSpec as P

LANES = 128
DEPTH_CUTS = 4
ROW_CUTS = 1
FREE = pl.CostEstimate(flops=0, bytes_accessed=0, transcendentals=0)
OWN_SPLITS = 2
PRODUCT_BYTES = 51 * 1024 * 1024
WHOLE_BYTES = 24 * 1024 * 1024
CUT_BYTES = 56 * 1024 * 1024
SUM_BYTES = 8 * 1024 * 1024


WHOLE = pl.BlockSpec(memory_space=pltpu.VMEM)


def passed_along(value, axis, steps):
    count = lax.axis_size(axis)
    pairs = [(source, (source + steps) % count) for source in range(count)]
    return lax.ppermute(value, axis, pairs)


def transpose_block(values, width):
    count = values.shape[0]
    return values.reshape(count, width, width).transpose(0, 2, 1).reshape(count, width * width)


def column_cuts(columns):
    half, quarter = columns // 2, columns // 4
    return [(0, half), (half, half + quarter), (half + quarter, columns)]


def after(value, earlier):
    return lax.optimization_barrier((value, earlier))[0]


def in_column_order(blocks, count):
    own = lax.axis_index("pair")
    ordered = []
    for place in range(count):
        block = blocks[place]
        for index in range(1, count):
            block = jnp.where(own == index, blocks[(place - index) % count], block)
        ordered.append(block)
    return jnp.concatenate(ordered, axis=1)


def add_product(a_refs, b_ref, total_ref, base_ref):
    columns = b_ref[...]
    rows = a_refs[0].shape[0]
    for index, a_ref in enumerate(a_refs):
        part = slice(index * rows, (index + 1) * rows)
        term = jnp.dot(a_ref[...], columns, preferred_element_type=jnp.float32)

        @pl.when(pl.program_id(0) == 0)
        def _():
            total_ref[part, :] = term if base_ref is None else term + base_ref[part, :]

        @pl.when(pl.program_id(0) > 0)
        def _():
            total_ref[part, :] += term


def row_blocks(rows, part, first):
    return [pl.BlockSpec((rows // ROW_CUTS, part), lambda k, j=j: (j, k + first)) for j in range(ROW_CUTS)]


def product_cost(rows, columns):
    depth, width = columns.shape
    return pl.CostEstimate(flops=2 * rows * depth * width, bytes_accessed=2 * rows * depth, transcendentals=0)


def product_kernel(steps, order, splits, has_base, bit_ref, *refs):
    a_refs, b_ref = refs[:ROW_CUTS], refs[ROW_CUTS]
    base_ref = refs[ROW_CUTS + 1] if has_base else None
    out_refs, total_ref = refs[-1 - 2 * splits : -1], refs[-1]
    step = pl.program_id(0)
    add_product(a_refs, b_ref, total_ref, base_ref)

    @pl.when(step == steps - 1)
    def _():
        rows, width = out_refs[0].shape
        rows = rows // len(order)
        for index, out_ref in enumerate(out_refs):
            bit = 1 - bit_ref[0] if index % 2 else bit_ref[0]
            columns = slice(index // 2 * width, (index // 2 + 1) * width)
            for place, block in enumerate(order):
                start = pl.multiple_of((block + bit) * rows, rows)
                out_ref[place * rows : (place + 1) * rows, :] = total_ref[pl.ds(start, rows), columns]


def multiplied(amplitudes, columns, bit, order, first=0, base=None, splits=1):
    rows, depth = amplitudes.shape
    width = columns.shape[1]
    part = depth // DEPTH_CUTS
    steps = columns.shape[0] // part
    shape = jax.ShapeDtypeStruct((rows // 2, width // splits), jnp.float32)
    bases = [] if base is None else [base]
    return pl.pallas_call(
        functools.partial(product_kernel, steps, order, splits, base is not None),
        grid=(steps,),
        out_shape=[shape] * (2 * splits),
        in_specs=[
            pl.BlockSpec(memory_space=pltpu.SMEM),
            *row_blocks(rows, part, first),
            pl.BlockSpec((part, width), lambda k: (k, 0)),
        ]
        + [pl.BlockSpec((rows, width), lambda k: (0, 0)) for _ in bases],
        out_specs=[pl.BlockSpec(shape.shape, lambda k: (0, 0))] * (2 * splits),
        scratch_shapes=[pltpu.VMEM((rows, width), jnp.float32)],
        compiler_params=pltpu.CompilerParams(vmem_limit_bytes=PRODUCT_BYTES),
        cost_estimate=product_cost(rows, columns) if splits == 1 else FREE,
    )(bit, *[amplitudes] * ROW_CUTS, columns, *bases)


def add_whole(a_ref, b_ref, total_ref, first, base_ref):
    depth = b_ref.shape[0]
    part = a_ref.shape[1] // DEPTH_CUTS
    for low in range(0, depth, part):
        term = jnp.dot(a_ref[:, first + low : first + low + part], b_ref[low : low + part, :], preferred_element_type=jnp.float32)
        if low > 0:
            total_ref[...] += term
        else:
            total_ref[...] = term if base_ref is None else base_ref[...] + term


def whole_kernel(order, first, has_base, bit_ref, a_ref, b_ref, *refs):
    keep_ref, send_ref, total_ref = refs[-3:]
    add_whole(a_ref, b_ref, total_ref, first, refs[0] if has_base else None)
    rows = keep_ref.shape[0] // len(order)
    for out_ref, bit in ((keep_ref, bit_ref[0]), (send_ref, 1 - bit_ref[0])):
        for place, block in enumerate(order):
            start = pl.multiple_of((block + bit) * rows, rows)
            out_ref[place * rows : (place + 1) * rows, :] = total_ref[pl.ds(start, rows), :]


def whole_multiplied(amplitudes, columns, bit, order, first=0, base=None):
    rows = amplitudes.shape[0]
    width = columns.shape[1]
    bases = [] if base is None else [base]
    return pl.pallas_call(
        functools.partial(whole_kernel, order, first, base is not None),
        out_shape=[jax.ShapeDtypeStruct((rows // 2, width), jnp.float32)] * 2,
        in_specs=[pl.BlockSpec(memory_space=pltpu.SMEM)] + [WHOLE] * (2 + len(bases)),
        out_specs=[WHOLE] * 2,
        scratch_shapes=[pltpu.VMEM((rows, width), jnp.float32)],
        compiler_params=pltpu.CompilerParams(vmem_limit_bytes=WHOLE_BYTES),
        cost_estimate=product_cost(rows, columns),
    )(bit, amplitudes, columns, *bases)


def whole_plain_kernel(a_ref, b_ref, out_ref):
    add_whole(a_ref, b_ref, out_ref, 0, None)


def whole_plain(amplitudes, columns):
    rows = amplitudes.shape[0]
    return pl.pallas_call(
        whole_plain_kernel,
        out_shape=jax.ShapeDtypeStruct((rows, columns.shape[1]), jnp.float32),
        in_specs=[WHOLE] * 2,
        out_specs=WHOLE,
        compiler_params=pltpu.CompilerParams(vmem_limit_bytes=WHOLE_BYTES),
        cost_estimate=product_cost(rows, columns),
    )(amplitudes, columns)


def halve_kernel(bit_ref, mine_ref, came_ref, keep_ref, send_ref):
    rows = keep_ref.shape[0]
    for out_ref, bit in ((keep_ref, bit_ref[0]), (send_ref, 1 - bit_ref[0])):
        part = pl.ds(pl.multiple_of(bit * rows, rows), rows)
        out_ref[...] = mine_ref[part, :] + came_ref[part, :]


def halved(mine, came, bit):
    rows, width = mine.shape
    shape = jax.ShapeDtypeStruct((rows // 2, width), jnp.float32)
    return pl.pallas_call(
        halve_kernel,
        out_shape=[shape] * 2,
        in_specs=[pl.BlockSpec(memory_space=pltpu.SMEM)] + [pl.BlockSpec(memory_space=pltpu.VMEM)] * 2,
        out_specs=[pl.BlockSpec(memory_space=pltpu.VMEM)] * 2,
        compiler_params=pltpu.CompilerParams(vmem_limit_bytes=SUM_BYTES),
        cost_estimate=FREE,
    )(bit, mine, came)


def flipped_along(value, axis, bits):
    count = lax.axis_size(axis)
    return lax.ppermute(value, axis, [(source, source ^ bits) for source in range(count)])


def exchanged_sum(parts, bits, gates=()):
    stages = []
    for level in range(1, len(bits)):
        keep, send = parts
        came = flipped_along(send, "virt", 1 << (level - 1))
        if level in gates:
            came = after(came, gates[level])
        parts = halved(keep, came, bits[level]) if level < len(bits) - 1 else [keep + came]
        stages.append(parts[0])
    return (parts[0], flipped_along(parts[0], "virt", 1 << (len(bits) - 1))), stages


def cut_kernel(boxes, source_ref, *refs):
    copies = []
    for index, (rows, columns) in enumerate(boxes):
        part = (rows[1] - rows[0]) // DEPTH_CUTS
        for low in range(0, rows[1] - rows[0], part):
            source = source_ref.at[rows[0] + low : rows[0] + low + part, columns[0] : columns[1]]
            target = refs[index].at[low : low + part, :]
            copies.append(pltpu.make_async_copy(source, target, refs[-1].at[len(copies)]))
    for copy in copies:
        copy.start()
    for copy in copies:
        copy.wait()


def cut_out(source, rows, columns):
    if columns[0] % LANES or columns[1] % LANES:
        return source[rows[0] : rows[1], columns[0] : columns[1]]
    return pl.pallas_call(
        functools.partial(cut_kernel, [(rows, columns)]),
        out_shape=[jax.ShapeDtypeStruct((rows[1] - rows[0], columns[1] - columns[0]), source.dtype)],
        in_specs=[pl.BlockSpec(memory_space=pl.ANY)],
        out_specs=[WHOLE],
        scratch_shapes=[pltpu.SemaphoreType.DMA((DEPTH_CUTS,))],
        compiler_params=pltpu.CompilerParams(vmem_limit_bytes=CUT_BYTES),
        cost_estimate=FREE,
    )(source)[0]


def last_kernel(width, starts, where_ref, rows_ref, virt_ref, occ_ref, *refs):
    blocks, (out_ref, both_ref, tall_ref, turned_ref) = refs[:-4], refs[-4:]
    rows = out_ref.shape[0]
    for index, start in enumerate(starts):
        value = blocks[index][...]
        if index == len(starts) - 1:
            value = value + blocks[index + 1][...]
        columns = out_ref.shape[1] // 2
        side = where_ref[1] if start < columns else 1 - where_ref[1]
        place = pl.multiple_of(side * columns + start % columns, LANES)
        both_ref[:, pl.ds(place, value.shape[1])] = value
    upper = where_ref[0]
    mine = both_ref[pl.ds(pl.multiple_of(upper * rows, rows), rows), :]
    other = both_ref[pl.ds(pl.multiple_of((1 - upper) * rows, rows), rows), :]
    chosen = (rows_ref[...] == lax.broadcasted_iota(jnp.int32, (rows, rows), 1)).astype(jnp.float32)
    flipped = jnp.dot(chosen, other, precision=lax.Precision.HIGHEST, preferred_element_type=jnp.float32)
    tall_ref[...] = flipped.T
    for b in range(width):
        turned_ref[b * width : (b + 1) * width, :] = tall_ref[pl.ds(b, width, stride=width), :]
    out_ref[...] = (mine + turned_ref[...].T) / (virt_ref[...] - occ_ref[...])


def last_steps(blocks, where, local_rows, virt_sum, occ_sum, width):
    rows = occ_sum.shape[0]
    columns = virt_sum.shape[0]
    starts, start = [], 0
    for block in blocks[:-1]:
        starts.append(start)
        start += block.shape[1]
    return pl.pallas_call(
        functools.partial(last_kernel, width, starts),
        out_shape=jax.ShapeDtypeStruct((rows, columns), jnp.float32),
        in_specs=[pl.BlockSpec(memory_space=pltpu.SMEM)] + [WHOLE] * (3 + len(blocks)),
        out_specs=WHOLE,
        scratch_shapes=[
            pltpu.VMEM((2 * rows, columns), jnp.float32),
            pltpu.VMEM((columns, rows), jnp.float32),
            pltpu.VMEM((columns, rows), jnp.float32),
        ],
        compiler_params=pltpu.CompilerParams(vmem_limit_bytes=SUM_BYTES),
        cost_estimate=FREE,
    )(where, local_rows.reshape(rows, 1), virt_sum.reshape(1, columns), occ_sum.reshape(rows, 1), *blocks)


def per_device(amplitudes, integrals, occ_pairs, partners, virt_list, eps_occ, eps_virt):
    width = virt_list.shape[0]
    count = lax.axis_size("pair")
    size = lax.axis_size("virt")
    rows = amplitudes.shape[0] // size
    cuts = column_cuts(integrals.shape[1])
    me = lax.axis_index("virt").astype(jnp.int32)
    levels = size.bit_length() - 1
    bits = [((me >> level) & 1).reshape(1) for level in range(levels)]
    order = [sum(((place >> (levels - 1 - level)) & 1) << level for level in range(1, levels)) for place in range(size // 2)]
    upper = me >= size // 2

    def sent(piece):
        return [passed_along(piece, "pair", -shift) for shift in range(1, count)]

    depth = integrals.shape[0]
    late = depth // DEPTH_CUTS * (DEPTH_CUTS - 1)
    first = cut_out(integrals, (0, depth), cuts[0])
    rest = after(integrals, first)
    low, high = cuts[-1]
    pieces = [first] + [rest[:, low:high] for low, high in cuts[1:-1]] + [rest[:late, low:high], rest[late:, low:high]]
    in_flight = [sent(pieces[0]), sent(pieces[1])]
    own_product = multiplied(amplitudes, after(rest, pieces), bits[0], order, splits=OWN_SPLITS)
    own_sums = [jnp.add(*exchanged_sum(own_product[2 * part : 2 * part + 2], bits)[0]) for part in range(OWN_SPLITS)]
    sums = [own_sums] + [[] for _ in range(1, count)]
    in_flight += [sent(after(piece, own_sums)) for piece in pieces[2:]]
    earlier, gates = own_sums, {}
    for step in range(len(pieces)):
        arrived, earlier = lax.optimization_barrier((in_flight[step], earlier))
        if step == len(pieces) - 2:
            bases = [whole_plain(amplitudes, columns) for columns in arrived]
            earlier = (stages[2], bases)
            continue
        for shift in range(1, count):
            if step < len(cuts) - 1:
                product = multiplied(amplitudes, arrived[shift - 1], bits[0], order)
            else:
                product = whole_multiplied(amplitudes, arrived[shift - 1], bits[0], order, late, bases[shift - 1])
            terms, stages = exchanged_sum(product, bits, gates)
            total = jnp.add(*terms)
            sums[shift].append(total)
            earlier, gates = stages[2] if step < len(cuts) - 2 else stages[0], {2: total}

    occ_ids = jnp.arange(eps_occ.shape[0], dtype=jnp.int32)
    occ_match = occ_pairs[:, :, None] == occ_ids[None, None, :]
    occ_sum = jnp.sum(jnp.where(occ_match, eps_occ[None, None, :], 0.0), axis=(1, 2))
    virt_ids = jnp.arange(eps_virt.shape[0], dtype=jnp.int32)
    virt_match = virt_list[:, None] == virt_ids[None, :]
    virt_energy = jnp.sum(jnp.where(virt_match, eps_virt[None, :], 0.0), axis=1)
    virt_sum = (virt_energy[:, None] + virt_energy[None, :]).reshape(-1)
    if count == 2 and all(block.shape[1] % LANES == 0 for parts in sums for block in parts):
        where = jnp.stack([upper.astype(jnp.int32), lax.axis_index("pair").astype(jnp.int32)])
        blocks = [*sums[0], *sums[1][:-1], *terms]
        return last_steps(blocks, where, partners % rows, virt_sum, occ_sum, width)
    both = in_column_order([jnp.concatenate(parts, axis=1) for parts in sums], count)
    mine = jnp.where(upper, both[rows:], both[:rows])
    other = jnp.where(upper, both[:rows], both[rows:])
    flipped = jnp.take(other, partners % mine.shape[0], axis=0)
    total = mine + transpose_block(flipped, width)

    denominator = virt_sum[None, :] - occ_sum[:, None]
    return total / denominator


def solution(mesh):
    placed = (
        P("pair", "virt"),
        P("virt", "pair"),
        P(("pair", "virt"), None),
        P(("pair", "virt")),
        P(),
        P(),
        P(),
    )
    return jax.shard_map(
        per_device, mesh=mesh, in_specs=placed, out_specs=P(("pair", "virt"), None), check_vma=False
    )
```

```python
import functools

import jax
import jax.numpy as jnp
from jax import lax
from jax.experimental import pallas as pl
from jax.experimental.pallas import tpu as pltpu
from jax.sharding import PartitionSpec as P

LANES = 128
DEPTH_CUTS = 4
CUT_STEPS = 8
ROW_STEPS = 4
ROW_CUTS = 1
FREE = pl.CostEstimate(flops=0, bytes_accessed=0, transcendentals=0)
OWN_SPLITS = 2
PRODUCT_BYTES = 51 * 1024 * 1024
WHOLE_BYTES = 24 * 1024 * 1024
CUT_BYTES = 56 * 1024 * 1024
SUM_BYTES = 8 * 1024 * 1024


WHOLE = pl.BlockSpec(memory_space=pltpu.VMEM)


def passed_along(value, axis, steps):
    count = lax.axis_size(axis)
    pairs = [(source, (source + steps) % count) for source in range(count)]
    return lax.ppermute(value, axis, pairs)


def transpose_block(values, width):
    count = values.shape[0]
    return values.reshape(count, width, width).transpose(0, 2, 1).reshape(count, width * width)


def column_cuts(columns):
    half, quarter = columns // 2, columns // 4
    return [(0, half), (half, half + quarter), (half + quarter, columns)]


def after(value, earlier):
    return lax.optimization_barrier((value, earlier))[0]


def in_column_order(blocks, count):
    own = lax.axis_index("pair")
    ordered = []
    for place in range(count):
        block = blocks[place]
        for index in range(1, count):
            block = jnp.where(own == index, blocks[(place - index) % count], block)
        ordered.append(block)
    return jnp.concatenate(ordered, axis=1)


def add_product(a_refs, b_ref, total_ref, base_ref):
    columns = b_ref[...]
    rows = a_refs[0].shape[0]
    for index, a_ref in enumerate(a_refs):
        part = slice(index * rows, (index + 1) * rows)
        term = jnp.dot(a_ref[...], columns, preferred_element_type=jnp.float32)

        @pl.when(pl.program_id(0) == 0)
        def _():
            total_ref[part, :] = term if base_ref is None else term + base_ref[part, :]

        @pl.when(pl.program_id(0) > 0)
        def _():
            total_ref[part, :] += term


def row_blocks(rows, part, first):
    return [pl.BlockSpec((rows // ROW_CUTS, part), lambda k, j=j: (j, k + first)) for j in range(ROW_CUTS)]


def product_cost(rows, columns):
    depth, width = columns.shape
    return pl.CostEstimate(flops=2 * rows * depth * width, bytes_accessed=2 * rows * depth, transcendentals=0)


def product_kernel(steps, order, splits, has_base, bit_ref, *refs):
    a_refs, b_ref = refs[:ROW_CUTS], refs[ROW_CUTS]
    base_ref = refs[ROW_CUTS + 1] if has_base else None
    out_refs, total_ref = refs[-1 - 2 * splits : -1], refs[-1]
    step = pl.program_id(0)
    add_product(a_refs, b_ref, total_ref, base_ref)

    @pl.when(step == steps - 1)
    def _():
        rows, width = out_refs[0].shape
        rows = rows // len(order)
        for index, out_ref in enumerate(out_refs):
            bit = 1 - bit_ref[0] if index % 2 else bit_ref[0]
            columns = slice(index // 2 * width, (index // 2 + 1) * width)
            for place, block in enumerate(order):
                start = pl.multiple_of((block + bit) * rows, rows)
                out_ref[place * rows : (place + 1) * rows, :] = total_ref[pl.ds(start, rows), columns]


def multiplied(amplitudes, columns, bit, order, first=0, base=None, splits=1):
    rows, depth = amplitudes.shape
    width = columns.shape[1]
    part = depth // DEPTH_CUTS
    steps = columns.shape[0] // part
    shape = jax.ShapeDtypeStruct((rows // 2, width // splits), jnp.float32)
    bases = [] if base is None else [base]
    return pl.pallas_call(
        functools.partial(product_kernel, steps, order, splits, base is not None),
        grid=(steps,),
        out_shape=[shape] * (2 * splits),
        in_specs=[
            pl.BlockSpec(memory_space=pltpu.SMEM),
            *row_blocks(rows, part, first),
            pl.BlockSpec((part, width), lambda k: (k, 0)),
        ]
        + [pl.BlockSpec((rows, width), lambda k: (0, 0)) for _ in bases],
        out_specs=[pl.BlockSpec(shape.shape, lambda k: (0, 0))] * (2 * splits),
        scratch_shapes=[pltpu.VMEM((rows, width), jnp.float32)],
        compiler_params=pltpu.CompilerParams(vmem_limit_bytes=PRODUCT_BYTES),
        cost_estimate=product_cost(rows, columns) if splits == 1 else FREE,
    )(bit, *[amplitudes] * ROW_CUTS, columns, *bases)


def rowwise_kernel(steps, order, bit_ref, a_ref, b_ref, keep_ref, send_ref, total_ref):
    step = pl.program_id(0)
    rows = a_ref.shape[0]
    term = jnp.dot(a_ref[...], b_ref[...], preferred_element_type=jnp.float32)
    total_ref[pl.ds(pl.multiple_of(step * rows, rows), rows), :] = term

    @pl.when(step == steps - 1)
    def _():
        share_out(order, bit_ref, total_ref, keep_ref, send_ref)


def share_out(order, bit_ref, total_ref, keep_ref, send_ref):
    rows = keep_ref.shape[0] // len(order)
    for out_ref, bit in ((keep_ref, bit_ref[0]), (send_ref, 1 - bit_ref[0])):
        for place, block in enumerate(order):
            start = pl.multiple_of((block + bit) * rows, rows)
            out_ref[place * rows : (place + 1) * rows, :] = total_ref[pl.ds(start, rows), :]


def rowwise_multiplied(amplitudes, columns, bit, order):
    rows, depth = amplitudes.shape
    width = columns.shape[1]
    shape = jax.ShapeDtypeStruct((rows // 2, width), jnp.float32)
    return pl.pallas_call(
        functools.partial(rowwise_kernel, ROW_STEPS, order),
        grid=(ROW_STEPS,),
        out_shape=[shape] * 2,
        in_specs=[
            pl.BlockSpec(memory_space=pltpu.SMEM),
            pl.BlockSpec((rows // ROW_STEPS, depth), lambda m: (m, 0)),
            pl.BlockSpec((depth, width), lambda m: (0, 0)),
        ],
        out_specs=[pl.BlockSpec(shape.shape, lambda m: (0, 0))] * 2,
        scratch_shapes=[pltpu.VMEM((rows, width), jnp.float32)],
        compiler_params=pltpu.CompilerParams(vmem_limit_bytes=PRODUCT_BYTES),
        cost_estimate=product_cost(rows, columns),
    )(bit, amplitudes, columns)


def add_whole(a_ref, b_ref, total_ref, first, base_ref):
    depth = b_ref.shape[0]
    part = a_ref.shape[1] // DEPTH_CUTS
    for low in range(0, depth, part):
        term = jnp.dot(a_ref[:, first + low : first + low + part], b_ref[low : low + part, :], preferred_element_type=jnp.float32)
        if low > 0:
            total_ref[...] += term
        else:
            total_ref[...] = term if base_ref is None else base_ref[...] + term


def whole_kernel(order, first, has_base, bit_ref, a_ref, b_ref, *refs):
    keep_ref, send_ref, total_ref = refs[-3:]
    add_whole(a_ref, b_ref, total_ref, first, refs[0] if has_base else None)
    share_out(order, bit_ref, total_ref, keep_ref, send_ref)


def whole_multiplied(amplitudes, columns, bit, order, first=0, base=None):
    rows = amplitudes.shape[0]
    width = columns.shape[1]
    bases = [] if base is None else [base]
    return pl.pallas_call(
        functools.partial(whole_kernel, order, first, base is not None),
        out_shape=[jax.ShapeDtypeStruct((rows // 2, width), jnp.float32)] * 2,
        in_specs=[pl.BlockSpec(memory_space=pltpu.SMEM)] + [WHOLE] * (2 + len(bases)),
        out_specs=[WHOLE] * 2,
        scratch_shapes=[pltpu.VMEM((rows, width), jnp.float32)],
        compiler_params=pltpu.CompilerParams(vmem_limit_bytes=WHOLE_BYTES),
        cost_estimate=product_cost(rows, columns),
    )(bit, amplitudes, columns, *bases)


def whole_plain_kernel(a_ref, b_ref, out_ref):
    add_whole(a_ref, b_ref, out_ref, 0, None)


def whole_plain(amplitudes, columns):
    rows = amplitudes.shape[0]
    return pl.pallas_call(
        whole_plain_kernel,
        out_shape=jax.ShapeDtypeStruct((rows, columns.shape[1]), jnp.float32),
        in_specs=[WHOLE] * 2,
        out_specs=WHOLE,
        compiler_params=pltpu.CompilerParams(vmem_limit_bytes=WHOLE_BYTES),
        cost_estimate=product_cost(rows, columns),
    )(amplitudes, columns)


def halve_kernel(bit_ref, mine_ref, came_ref, keep_ref, send_ref):
    rows = keep_ref.shape[0]
    for out_ref, bit in ((keep_ref, bit_ref[0]), (send_ref, 1 - bit_ref[0])):
        part = pl.ds(pl.multiple_of(bit * rows, rows), rows)
        out_ref[...] = mine_ref[part, :] + came_ref[part, :]


def halved(mine, came, bit):
    rows, width = mine.shape
    shape = jax.ShapeDtypeStruct((rows // 2, width), jnp.float32)
    return pl.pallas_call(
        halve_kernel,
        out_shape=[shape] * 2,
        in_specs=[pl.BlockSpec(memory_space=pltpu.SMEM)] + [pl.BlockSpec(memory_space=pltpu.VMEM)] * 2,
        out_specs=[pl.BlockSpec(memory_space=pltpu.VMEM)] * 2,
        compiler_params=pltpu.CompilerParams(vmem_limit_bytes=SUM_BYTES),
        cost_estimate=FREE,
    )(bit, mine, came)


def flipped_along(value, axis, bits):
    count = lax.axis_size(axis)
    return lax.ppermute(value, axis, [(source, source ^ bits) for source in range(count)])


def exchanged_sum(parts, bits, gates=()):
    stages = []
    for level in range(1, len(bits)):
        keep, send = parts
        came = flipped_along(send, "virt", 1 << (level - 1))
        if level in gates:
            came = after(came, gates[level])
        parts = halved(keep, came, bits[level]) if level < len(bits) - 1 else [keep + came]
        stages.append(parts[0])
    return (parts[0], flipped_along(parts[0], "virt", 1 << (len(bits) - 1))), stages


def cut_kernel(source_ref, piece_ref):
    piece_ref[...] = source_ref[...]


def first_columns(source, width):
    if width % LANES:
        return source[:, :width]
    depth = source.shape[0]
    block = pl.BlockSpec((depth // CUT_STEPS, width), lambda k: (k, 0))
    return pl.pallas_call(
        cut_kernel,
        grid=(CUT_STEPS,),
        out_shape=jax.ShapeDtypeStruct((depth, width), source.dtype),
        in_specs=[block],
        out_specs=block,
        compiler_params=pltpu.CompilerParams(vmem_limit_bytes=CUT_BYTES),
        cost_estimate=FREE,
    )(source)


def last_kernel(width, starts, where_ref, rows_ref, virt_ref, occ_ref, *refs):
    blocks, (out_ref, both_ref, tall_ref, turned_ref) = refs[:-4], refs[-4:]
    rows = out_ref.shape[0]
    for index, start in enumerate(starts):
        value = blocks[index][...]
        if index == len(starts) - 1:
            value = value + blocks[index + 1][...]
        columns = out_ref.shape[1] // 2
        side = where_ref[1] if start < columns else 1 - where_ref[1]
        place = pl.multiple_of(side * columns + start % columns, LANES)
        both_ref[:, pl.ds(place, value.shape[1])] = value
    upper = where_ref[0]
    mine = both_ref[pl.ds(pl.multiple_of(upper * rows, rows), rows), :]
    other = both_ref[pl.ds(pl.multiple_of((1 - upper) * rows, rows), rows), :]
    chosen = (rows_ref[...] == lax.broadcasted_iota(jnp.int32, (rows, rows), 1)).astype(jnp.float32)
    flipped = jnp.dot(chosen, other, precision=lax.Precision.HIGHEST, preferred_element_type=jnp.float32)
    tall_ref[...] = flipped.T
    for b in range(width):
        turned_ref[b * width : (b + 1) * width, :] = tall_ref[pl.ds(b, width, stride=width), :]
    out_ref[...] = (mine + turned_ref[...].T) / (virt_ref[...] - occ_ref[...])


def last_steps(blocks, where, local_rows, virt_sum, occ_sum, width):
    rows = occ_sum.shape[0]
    columns = virt_sum.shape[0]
    starts, start = [], 0
    for block in blocks[:-1]:
        starts.append(start)
        start += block.shape[1]
    return pl.pallas_call(
        functools.partial(last_kernel, width, starts),
        out_shape=jax.ShapeDtypeStruct((rows, columns), jnp.float32),
        in_specs=[pl.BlockSpec(memory_space=pltpu.SMEM)] + [WHOLE] * (3 + len(blocks)),
        out_specs=WHOLE,
        scratch_shapes=[
            pltpu.VMEM((2 * rows, columns), jnp.float32),
            pltpu.VMEM((columns, rows), jnp.float32),
            pltpu.VMEM((columns, rows), jnp.float32),
        ],
        compiler_params=pltpu.CompilerParams(vmem_limit_bytes=SUM_BYTES),
        cost_estimate=FREE,
    )(where, local_rows.reshape(rows, 1), virt_sum.reshape(1, columns), occ_sum.reshape(rows, 1), *blocks)


def per_device(amplitudes, integrals, occ_pairs, partners, virt_list, eps_occ, eps_virt):
    width = virt_list.shape[0]
    count = lax.axis_size("pair")
    size = lax.axis_size("virt")
    rows = amplitudes.shape[0] // size
    cuts = column_cuts(integrals.shape[1])
    me = lax.axis_index("virt").astype(jnp.int32)
    levels = size.bit_length() - 1
    bits = [((me >> level) & 1).reshape(1) for level in range(levels)]
    order = [sum(((place >> (levels - 1 - level)) & 1) << level for level in range(1, levels)) for place in range(size // 2)]
    upper = me >= size // 2

    def sent(piece):
        return [passed_along(piece, "pair", -shift) for shift in range(1, count)]

    depth = integrals.shape[0]
    late = depth // DEPTH_CUTS * (DEPTH_CUTS - 1)
    first = first_columns(integrals, cuts[0][1])
    rest = after(integrals, first)
    low, high = cuts[-1]
    pieces = [first] + [rest[:, low:high] for low, high in cuts[1:-1]] + [rest[:late, low:high], rest[late:, low:high]]
    in_flight = [sent(pieces[0]), sent(pieces[1])]
    own_product = multiplied(amplitudes, after(rest, pieces), bits[0], order, splits=OWN_SPLITS)
    own_sums = [jnp.add(*exchanged_sum(own_product[2 * part : 2 * part + 2], bits)[0]) for part in range(OWN_SPLITS)]
    sums = [own_sums] + [[] for _ in range(1, count)]
    in_flight += [sent(after(piece, own_sums)) for piece in pieces[2:]]
    earlier, gates = own_sums, {}
    for step in range(len(pieces)):
        arrived, earlier = lax.optimization_barrier((in_flight[step], earlier))
        if step == len(pieces) - 2:
            bases = [whole_plain(amplitudes, columns) for columns in arrived]
            earlier = (stages[2], bases)
            continue
        for shift in range(1, count):
            if step < len(cuts) - 1:
                product = rowwise_multiplied(amplitudes, arrived[shift - 1], bits[0], order)
            else:
                product = whole_multiplied(amplitudes, arrived[shift - 1], bits[0], order, late, bases[shift - 1])
            terms, stages = exchanged_sum(product, bits, gates)
            total = jnp.add(*terms)
            sums[shift].append(total)
            earlier, gates = stages[2] if step < len(cuts) - 2 else stages[0], {2: total}

    occ_ids = jnp.arange(eps_occ.shape[0], dtype=jnp.int32)
    occ_match = occ_pairs[:, :, None] == occ_ids[None, None, :]
    occ_sum = jnp.sum(jnp.where(occ_match, eps_occ[None, None, :], 0.0), axis=(1, 2))
    virt_ids = jnp.arange(eps_virt.shape[0], dtype=jnp.int32)
    virt_match = virt_list[:, None] == virt_ids[None, :]
    virt_energy = jnp.sum(jnp.where(virt_match, eps_virt[None, :], 0.0), axis=1)
    virt_sum = (virt_energy[:, None] + virt_energy[None, :]).reshape(-1)
    if count == 2 and all(block.shape[1] % LANES == 0 for parts in sums for block in parts):
        where = jnp.stack([upper.astype(jnp.int32), lax.axis_index("pair").astype(jnp.int32)])
        blocks = [*sums[0], *sums[1][:-1], *terms]
        return last_steps(blocks, where, partners % rows, virt_sum, occ_sum, width)
    both = in_column_order([jnp.concatenate(parts, axis=1) for parts in sums], count)
    mine = jnp.where(upper, both[rows:], both[:rows])
    other = jnp.where(upper, both[:rows], both[rows:])
    flipped = jnp.take(other, partners % mine.shape[0], axis=0)
    total = mine + transpose_block(flipped, width)

    denominator = virt_sum[None, :] - occ_sum[:, None]
    return total / denominator


def solution(mesh):
    placed = (
        P("pair", "virt"),
        P("virt", "pair"),
        P(("pair", "virt"), None),
        P(("pair", "virt")),
        P(),
        P(),
        P(),
    )
    return jax.shard_map(
        per_device, mesh=mesh, in_specs=placed, out_specs=P(("pair", "virt"), None), check_vma=False
    )
```

```python
import functools

import jax
import jax.numpy as jnp
from jax import lax
from jax.experimental import pallas as pl
from jax.experimental.pallas import tpu as pltpu
from jax.sharding import PartitionSpec as P

LANES = 128
DEPTH_CUTS = 4
ROW_CUTS = 1
FREE = pl.CostEstimate(flops=0, bytes_accessed=0, transcendentals=0)
OWN_SPLITS = 2
PRODUCT_BYTES = 51 * 1024 * 1024
WHOLE_BYTES = 24 * 1024 * 1024
CUT_BYTES = 56 * 1024 * 1024
SUM_BYTES = 8 * 1024 * 1024


WHOLE = pl.BlockSpec(memory_space=pltpu.VMEM)


def passed_along(value, axis, steps):
    count = lax.axis_size(axis)
    pairs = [(source, (source + steps) % count) for source in range(count)]
    return lax.ppermute(value, axis, pairs)


def transpose_block(values, width):
    count = values.shape[0]
    return values.reshape(count, width, width).transpose(0, 2, 1).reshape(count, width * width)


def column_cuts(columns):
    half, quarter = columns // 2, columns // 4
    return [(0, half), (half, half + quarter), (half + quarter, columns)]


def after(value, earlier):
    return lax.optimization_barrier((value, earlier))[0]


def in_column_order(blocks, count):
    own = lax.axis_index("pair")
    ordered = []
    for place in range(count):
        block = blocks[place]
        for index in range(1, count):
            block = jnp.where(own == index, blocks[(place - index) % count], block)
        ordered.append(block)
    return jnp.concatenate(ordered, axis=1)


def add_product(a_refs, b_ref, total_ref, base_ref):
    columns = b_ref[...]
    rows = a_refs[0].shape[0]
    for index, a_ref in enumerate(a_refs):
        part = slice(index * rows, (index + 1) * rows)
        term = jnp.dot(a_ref[...], columns, preferred_element_type=jnp.float32)

        @pl.when(pl.program_id(0) == 0)
        def _():
            total_ref[part, :] = term if base_ref is None else term + base_ref[part, :]

        @pl.when(pl.program_id(0) > 0)
        def _():
            total_ref[part, :] += term


def row_blocks(rows, part, first):
    return [pl.BlockSpec((rows // ROW_CUTS, part), lambda k, j=j: (j, k + first)) for j in range(ROW_CUTS)]


def product_cost(rows, columns):
    depth, width = columns.shape
    return pl.CostEstimate(flops=2 * rows * depth * width, bytes_accessed=2 * rows * depth, transcendentals=0)


def product_kernel(steps, order, splits, has_base, bit_ref, *refs):
    a_refs, b_ref = refs[:ROW_CUTS], refs[ROW_CUTS]
    base_ref = refs[ROW_CUTS + 1] if has_base else None
    out_refs, total_ref = refs[-1 - 2 * splits : -1], refs[-1]
    step = pl.program_id(0)
    add_product(a_refs, b_ref, total_ref, base_ref)

    @pl.when(step == steps - 1)
    def _():
        rows, width = out_refs[0].shape
        rows = rows // len(order)
        for index, out_ref in enumerate(out_refs):
            bit = 1 - bit_ref[0] if index % 2 else bit_ref[0]
            columns = slice(index // 2 * width, (index // 2 + 1) * width)
            for place, block in enumerate(order):
                start = pl.multiple_of((block + bit) * rows, rows)
                out_ref[place * rows : (place + 1) * rows, :] = total_ref[pl.ds(start, rows), columns]


def multiplied(amplitudes, columns, bit, order, first=0, base=None, splits=1):
    rows, depth = amplitudes.shape
    width = columns.shape[1]
    part = depth // DEPTH_CUTS
    steps = columns.shape[0] // part
    shape = jax.ShapeDtypeStruct((rows // 2, width // splits), jnp.float32)
    bases = [] if base is None else [base]
    return pl.pallas_call(
        functools.partial(product_kernel, steps, order, splits, base is not None),
        grid=(steps,),
        out_shape=[shape] * (2 * splits),
        in_specs=[
            pl.BlockSpec(memory_space=pltpu.SMEM),
            *row_blocks(rows, part, first),
            pl.BlockSpec((part, width), lambda k: (k, 0)),
        ]
        + [pl.BlockSpec((rows, width), lambda k: (0, 0)) for _ in bases],
        out_specs=[pl.BlockSpec(shape.shape, lambda k: (0, 0))] * (2 * splits),
        scratch_shapes=[pltpu.VMEM((rows, width), jnp.float32)],
        compiler_params=pltpu.CompilerParams(vmem_limit_bytes=PRODUCT_BYTES),
        cost_estimate=product_cost(rows, columns) if splits == 1 else FREE,
    )(bit, *[amplitudes] * ROW_CUTS, columns, *bases)


def add_whole(a_ref, b_ref, total_ref, first, base_ref):
    depth = b_ref.shape[0]
    part = a_ref.shape[1] // DEPTH_CUTS
    for low in range(0, depth, part):
        term = jnp.dot(a_ref[:, first + low : first + low + part], b_ref[low : low + part, :], preferred_element_type=jnp.float32)
        if low > 0:
            total_ref[...] += term
        else:
            total_ref[...] = term if base_ref is None else base_ref[...] + term


def whole_kernel(order, first, has_base, bit_ref, a_ref, b_ref, *refs):
    keep_ref, send_ref, total_ref = refs[-3:]
    add_whole(a_ref, b_ref, total_ref, first, refs[0] if has_base else None)
    rows = keep_ref.shape[0] // len(order)
    for out_ref, bit in ((keep_ref, bit_ref[0]), (send_ref, 1 - bit_ref[0])):
        for place, block in enumerate(order):
            start = pl.multiple_of((block + bit) * rows, rows)
            out_ref[place * rows : (place + 1) * rows, :] = total_ref[pl.ds(start, rows), :]


def whole_multiplied(amplitudes, columns, bit, order, first=0, base=None):
    rows = amplitudes.shape[0]
    width = columns.shape[1]
    bases = [] if base is None else [base]
    return pl.pallas_call(
        functools.partial(whole_kernel, order, first, base is not None),
        out_shape=[jax.ShapeDtypeStruct((rows // 2, width), jnp.float32)] * 2,
        in_specs=[pl.BlockSpec(memory_space=pltpu.SMEM)] + [WHOLE] * (2 + len(bases)),
        out_specs=[WHOLE] * 2,
        scratch_shapes=[pltpu.VMEM((rows, width), jnp.float32)],
        compiler_params=pltpu.CompilerParams(vmem_limit_bytes=WHOLE_BYTES),
        cost_estimate=product_cost(rows, columns),
    )(bit, amplitudes, columns, *bases)


def whole_plain_kernel(a_ref, b_ref, out_ref):
    add_whole(a_ref, b_ref, out_ref, 0, None)


def whole_plain(amplitudes, columns):
    rows = amplitudes.shape[0]
    return pl.pallas_call(
        whole_plain_kernel,
        out_shape=jax.ShapeDtypeStruct((rows, columns.shape[1]), jnp.float32),
        in_specs=[WHOLE] * 2,
        out_specs=WHOLE,
        compiler_params=pltpu.CompilerParams(vmem_limit_bytes=WHOLE_BYTES),
        cost_estimate=product_cost(rows, columns),
    )(amplitudes, columns)


def halve_kernel(bit_ref, mine_ref, came_ref, keep_ref, send_ref):
    rows = keep_ref.shape[0]
    for out_ref, bit in ((keep_ref, bit_ref[0]), (send_ref, 1 - bit_ref[0])):
        part = pl.ds(pl.multiple_of(bit * rows, rows), rows)
        out_ref[...] = mine_ref[part, :] + came_ref[part, :]


def halved(mine, came, bit):
    rows, width = mine.shape
    shape = jax.ShapeDtypeStruct((rows // 2, width), jnp.float32)
    return pl.pallas_call(
        halve_kernel,
        out_shape=[shape] * 2,
        in_specs=[pl.BlockSpec(memory_space=pltpu.SMEM)] + [pl.BlockSpec(memory_space=pltpu.VMEM)] * 2,
        out_specs=[pl.BlockSpec(memory_space=pltpu.VMEM)] * 2,
        compiler_params=pltpu.CompilerParams(vmem_limit_bytes=SUM_BYTES),
        cost_estimate=FREE,
    )(bit, mine, came)


def flipped_along(value, axis, bits):
    count = lax.axis_size(axis)
    return lax.ppermute(value, axis, [(source, source ^ bits) for source in range(count)])


def exchanged_sum(parts, bits, gates=()):
    stages = []
    for level in range(1, len(bits)):
        keep, send = parts
        came = flipped_along(send, "virt", 1 << (level - 1))
        if level in gates:
            came = after(came, gates[level])
        parts = halved(keep, came, bits[level]) if level < len(bits) - 1 else [keep + came]
        stages.append(parts[0])
    return (parts[0], flipped_along(parts[0], "virt", 1 << (len(bits) - 1))), stages


def cut_kernel(boxes, source_ref, *refs):
    copies = []
    for index, (rows, columns) in enumerate(boxes):
        part = (rows[1] - rows[0]) // DEPTH_CUTS
        for low in range(0, rows[1] - rows[0], part):
            source = source_ref.at[rows[0] + low : rows[0] + low + part, columns[0] : columns[1]]
            target = refs[index].at[low : low + part, :]
            copies.append(pltpu.make_async_copy(source, target, refs[-1].at[len(copies)]))
    for copy in copies:
        copy.start()
    for copy in copies:
        copy.wait()


def cut_out(source, boxes):
    if any(edge % LANES for _, columns in boxes for edge in columns):
        return [source[rows[0] : rows[1], columns[0] : columns[1]] for rows, columns in boxes]
    return pl.pallas_call(
        functools.partial(cut_kernel, boxes),
        out_shape=[jax.ShapeDtypeStruct((r[1] - r[0], c[1] - c[0]), source.dtype) for r, c in boxes],
        in_specs=[pl.BlockSpec(memory_space=pl.ANY)],
        out_specs=[WHOLE] * len(boxes),
        scratch_shapes=[pltpu.SemaphoreType.DMA((DEPTH_CUTS * len(boxes),))],
        compiler_params=pltpu.CompilerParams(vmem_limit_bytes=CUT_BYTES),
        cost_estimate=FREE,
    )(source)


def last_kernel(width, starts, where_ref, rows_ref, virt_ref, occ_ref, *refs):
    blocks, (out_ref, both_ref, tall_ref, turned_ref) = refs[:-4], refs[-4:]
    rows = out_ref.shape[0]
    for index, start in enumerate(starts):
        value = blocks[index][...]
        if index == len(starts) - 1:
            value = value + blocks[index + 1][...]
        columns = out_ref.shape[1] // 2
        side = where_ref[1] if start < columns else 1 - where_ref[1]
        place = pl.multiple_of(side * columns + start % columns, LANES)
        both_ref[:, pl.ds(place, value.shape[1])] = value
    upper = where_ref[0]
    mine = both_ref[pl.ds(pl.multiple_of(upper * rows, rows), rows), :]
    other = both_ref[pl.ds(pl.multiple_of((1 - upper) * rows, rows), rows), :]
    chosen = (rows_ref[...] == lax.broadcasted_iota(jnp.int32, (rows, rows), 1)).astype(jnp.float32)
    flipped = jnp.dot(chosen, other, precision=lax.Precision.HIGHEST, preferred_element_type=jnp.float32)
    tall_ref[...] = flipped.T
    for b in range(width):
        turned_ref[b * width : (b + 1) * width, :] = tall_ref[pl.ds(b, width, stride=width), :]
    out_ref[...] = (mine + turned_ref[...].T) / (virt_ref[...] - occ_ref[...])


def last_steps(blocks, where, local_rows, virt_sum, occ_sum, width):
    rows = occ_sum.shape[0]
    columns = virt_sum.shape[0]
    starts, start = [], 0
    for block in blocks[:-1]:
        starts.append(start)
        start += block.shape[1]
    return pl.pallas_call(
        functools.partial(last_kernel, width, starts),
        out_shape=jax.ShapeDtypeStruct((rows, columns), jnp.float32),
        in_specs=[pl.BlockSpec(memory_space=pltpu.SMEM)] + [WHOLE] * (3 + len(blocks)),
        out_specs=WHOLE,
        scratch_shapes=[
            pltpu.VMEM((2 * rows, columns), jnp.float32),
            pltpu.VMEM((columns, rows), jnp.float32),
            pltpu.VMEM((columns, rows), jnp.float32),
        ],
        compiler_params=pltpu.CompilerParams(vmem_limit_bytes=SUM_BYTES),
        cost_estimate=FREE,
    )(where, local_rows.reshape(rows, 1), virt_sum.reshape(1, columns), occ_sum.reshape(rows, 1), *blocks)


def per_device(amplitudes, integrals, occ_pairs, partners, virt_list, eps_occ, eps_virt):
    width = virt_list.shape[0]
    count = lax.axis_size("pair")
    size = lax.axis_size("virt")
    rows = amplitudes.shape[0] // size
    cuts = column_cuts(integrals.shape[1])
    me = lax.axis_index("virt").astype(jnp.int32)
    levels = size.bit_length() - 1
    bits = [((me >> level) & 1).reshape(1) for level in range(levels)]
    order = [sum(((place >> (levels - 1 - level)) & 1) << level for level in range(1, levels)) for place in range(size // 2)]
    upper = me >= size // 2

    def sent(piece):
        return [passed_along(piece, "pair", -shift) for shift in range(1, count)]

    depth = integrals.shape[0]
    late = depth // DEPTH_CUTS * (DEPTH_CUTS - 1)
    (first,) = cut_out(integrals, [((0, depth), cuts[0])])
    rest = after(integrals, first)
    boxes = [((0, depth), cut) for cut in cuts[1:-1]] + [((0, late), cuts[-1]), ((late, depth), cuts[-1])]
    pieces = [first, *cut_out(rest, boxes)]
    in_flight = [sent(pieces[0]), sent(pieces[1])]
    own_product = multiplied(amplitudes, after(rest, pieces), bits[0], order, splits=OWN_SPLITS)
    own_sums = [jnp.add(*exchanged_sum(own_product[2 * part : 2 * part + 2], bits)[0]) for part in range(OWN_SPLITS)]
    sums = [own_sums] + [[] for _ in range(1, count)]
    in_flight += [sent(after(piece, own_sums)) for piece in pieces[2:]]
    earlier, gates = own_sums, {}
    for step in range(len(pieces)):
        arrived, earlier = lax.optimization_barrier((in_flight[step], earlier))
        if step == len(pieces) - 2:
            bases = [whole_plain(amplitudes, columns) for columns in arrived]
            earlier = (stages[2], bases)
            continue
        for shift in range(1, count):
            if step < len(cuts) - 1:
                product = multiplied(amplitudes, arrived[shift - 1], bits[0], order)
            else:
                product = whole_multiplied(amplitudes, arrived[shift - 1], bits[0], order, late, bases[shift - 1])
            terms, stages = exchanged_sum(product, bits, gates)
            total = jnp.add(*terms)
            sums[shift].append(total)
            earlier, gates = stages[2] if step < len(cuts) - 2 else stages[0], {2: total}

    occ_ids = jnp.arange(eps_occ.shape[0], dtype=jnp.int32)
    occ_match = occ_pairs[:, :, None] == occ_ids[None, None, :]
    occ_sum = jnp.sum(jnp.where(occ_match, eps_occ[None, None, :], 0.0), axis=(1, 2))
    virt_ids = jnp.arange(eps_virt.shape[0], dtype=jnp.int32)
    virt_match = virt_list[:, None] == virt_ids[None, :]
    virt_energy = jnp.sum(jnp.where(virt_match, eps_virt[None, :], 0.0), axis=1)
    virt_sum = (virt_energy[:, None] + virt_energy[None, :]).reshape(-1)
    if count == 2 and all(block.shape[1] % LANES == 0 for parts in sums for block in parts):
        where = jnp.stack([upper.astype(jnp.int32), lax.axis_index("pair").astype(jnp.int32)])
        blocks = [*sums[0], *sums[1][:-1], *terms]
        return last_steps(blocks, where, partners % rows, virt_sum, occ_sum, width)
    both = in_column_order([jnp.concatenate(parts, axis=1) for parts in sums], count)
    mine = jnp.where(upper, both[rows:], both[:rows])
    other = jnp.where(upper, both[:rows], both[rows:])
    flipped = jnp.take(other, partners % mine.shape[0], axis=0)
    total = mine + transpose_block(flipped, width)

    denominator = virt_sum[None, :] - occ_sum[:, None]
    return total / denominator


def solution(mesh):
    placed = (
        P("pair", "virt"),
        P("virt", "pair"),
        P(("pair", "virt"), None),
        P(("pair", "virt")),
        P(),
        P(),
        P(),
    )
    return jax.shard_map(
        per_device, mesh=mesh, in_specs=placed, out_specs=P(("pair", "virt"), None), check_vma=False
    )
```

```python
import functools

import jax
import jax.numpy as jnp
from jax import lax
from jax.experimental import pallas as pl
from jax.experimental.pallas import tpu as pltpu
from jax.sharding import PartitionSpec as P

LANES = 128
DEPTH_CUTS = 4
ROW_CUTS = 1
FREE = pl.CostEstimate(flops=0, bytes_accessed=0, transcendentals=0)
OWN_SPLITS = 2
PRODUCT_BYTES = 51 * 1024 * 1024
WHOLE_BYTES = 24 * 1024 * 1024
CUT_BYTES = 56 * 1024 * 1024
SUM_BYTES = 8 * 1024 * 1024


WHOLE = pl.BlockSpec(memory_space=pltpu.VMEM)


def passed_along(value, axis, steps):
    count = lax.axis_size(axis)
    pairs = [(source, (source + steps) % count) for source in range(count)]
    return lax.ppermute(value, axis, pairs)


def transpose_block(values, width):
    count = values.shape[0]
    return values.reshape(count, width, width).transpose(0, 2, 1).reshape(count, width * width)


def column_cuts(columns):
    half, quarter = columns // 2, columns // 4
    return [(0, half), (half, half + quarter), (half + quarter, columns)]


def after(value, earlier):
    return lax.optimization_barrier((value, earlier))[0]


def in_column_order(blocks, count):
    own = lax.axis_index("pair")
    ordered = []
    for place in range(count):
        block = blocks[place]
        for index in range(1, count):
            block = jnp.where(own == index, blocks[(place - index) % count], block)
        ordered.append(block)
    return jnp.concatenate(ordered, axis=1)


def add_product(a_refs, b_ref, total_ref, base_ref):
    columns = b_ref[...]
    rows = a_refs[0].shape[0]
    for index, a_ref in enumerate(a_refs):
        part = slice(index * rows, (index + 1) * rows)
        term = jnp.dot(a_ref[...], columns, preferred_element_type=jnp.float32)

        @pl.when(pl.program_id(0) == 0)
        def _():
            total_ref[part, :] = term if base_ref is None else term + base_ref[part, :]

        @pl.when(pl.program_id(0) > 0)
        def _():
            total_ref[part, :] += term


def row_blocks(rows, part, first):
    return [pl.BlockSpec((rows // ROW_CUTS, part), lambda k, j=j: (j, k + first)) for j in range(ROW_CUTS)]


def product_cost(rows, columns):
    depth, width = columns.shape
    return pl.CostEstimate(flops=2 * rows * depth * width, bytes_accessed=2 * rows * depth, transcendentals=0)


def product_kernel(steps, order, splits, has_base, bit_ref, *refs):
    a_refs, b_ref = refs[:ROW_CUTS], refs[ROW_CUTS]
    base_ref = refs[ROW_CUTS + 1] if has_base else None
    out_refs, total_ref = refs[-1 - 2 * splits : -1], refs[-1]
    step = pl.program_id(0)
    add_product(a_refs, b_ref, total_ref, base_ref)

    @pl.when(step == steps - 1)
    def _():
        rows, width = out_refs[0].shape
        rows = rows // len(order)
        for index, out_ref in enumerate(out_refs):
            bit = 1 - bit_ref[0] if index % 2 else bit_ref[0]
            columns = slice(index // 2 * width, (index // 2 + 1) * width)
            for place, (even, odd) in enumerate(order):
                start = pl.multiple_of((even + bit * (odd - even + 1)) * rows, rows)
                out_ref[place * rows : (place + 1) * rows, :] = total_ref[pl.ds(start, rows), columns]


def multiplied(amplitudes, columns, bit, order, first=0, base=None, splits=1):
    rows, depth = amplitudes.shape
    width = columns.shape[1]
    part = depth // DEPTH_CUTS
    steps = columns.shape[0] // part
    shape = jax.ShapeDtypeStruct((rows // 2, width // splits), jnp.float32)
    bases = [] if base is None else [base]
    return pl.pallas_call(
        functools.partial(product_kernel, steps, order, splits, base is not None),
        grid=(steps,),
        out_shape=[shape] * (2 * splits),
        in_specs=[
            pl.BlockSpec(memory_space=pltpu.SMEM),
            *row_blocks(rows, part, first),
            pl.BlockSpec((part, width), lambda k: (k, 0)),
        ]
        + [pl.BlockSpec((rows, width), lambda k: (0, 0)) for _ in bases],
        out_specs=[pl.BlockSpec(shape.shape, lambda k: (0, 0))] * (2 * splits),
        scratch_shapes=[pltpu.VMEM((rows, width), jnp.float32)],
        compiler_params=pltpu.CompilerParams(vmem_limit_bytes=PRODUCT_BYTES),
        cost_estimate=product_cost(rows, columns) if splits == 1 else FREE,
    )(bit, *[amplitudes] * ROW_CUTS, columns, *bases)


def add_whole(a_ref, b_ref, total_ref, first, base_ref):
    depth = b_ref.shape[0]
    part = a_ref.shape[1] // DEPTH_CUTS
    for low in range(0, depth, part):
        term = jnp.dot(a_ref[:, first + low : first + low + part], b_ref[low : low + part, :], preferred_element_type=jnp.float32)
        if low > 0:
            total_ref[...] += term
        else:
            total_ref[...] = term if base_ref is None else base_ref[...] + term


def whole_kernel(order, first, has_base, bit_ref, a_ref, b_ref, *refs):
    keep_ref, send_ref, total_ref = refs[-3:]
    add_whole(a_ref, b_ref, total_ref, first, refs[0] if has_base else None)
    rows = keep_ref.shape[0] // len(order)
    for out_ref, bit in ((keep_ref, bit_ref[0]), (send_ref, 1 - bit_ref[0])):
        for place, (even, odd) in enumerate(order):
            start = pl.multiple_of((even + bit * (odd - even + 1)) * rows, rows)
            out_ref[place * rows : (place + 1) * rows, :] = total_ref[pl.ds(start, rows), :]


def whole_multiplied(amplitudes, columns, bit, order, first=0, base=None):
    rows = amplitudes.shape[0]
    width = columns.shape[1]
    bases = [] if base is None else [base]
    return pl.pallas_call(
        functools.partial(whole_kernel, order, first, base is not None),
        out_shape=[jax.ShapeDtypeStruct((rows // 2, width), jnp.float32)] * 2,
        in_specs=[pl.BlockSpec(memory_space=pltpu.SMEM)] + [WHOLE] * (2 + len(bases)),
        out_specs=[WHOLE] * 2,
        scratch_shapes=[pltpu.VMEM((rows, width), jnp.float32)],
        compiler_params=pltpu.CompilerParams(vmem_limit_bytes=WHOLE_BYTES),
        cost_estimate=product_cost(rows, columns),
    )(bit, amplitudes, columns, *bases)


def whole_plain_kernel(a_ref, b_ref, out_ref):
    add_whole(a_ref, b_ref, out_ref, 0, None)


def whole_plain(amplitudes, columns):
    rows = amplitudes.shape[0]
    return pl.pallas_call(
        whole_plain_kernel,
        out_shape=jax.ShapeDtypeStruct((rows, columns.shape[1]), jnp.float32),
        in_specs=[WHOLE] * 2,
        out_specs=WHOLE,
        compiler_params=pltpu.CompilerParams(vmem_limit_bytes=WHOLE_BYTES),
        cost_estimate=product_cost(rows, columns),
    )(amplitudes, columns)


def halve_kernel(bit_ref, mine_ref, came_ref, keep_ref, send_ref):
    rows = keep_ref.shape[0]
    for out_ref, bit in ((keep_ref, bit_ref[0]), (send_ref, 1 - bit_ref[0])):
        part = pl.ds(pl.multiple_of(bit * rows, rows), rows)
        out_ref[...] = mine_ref[part, :] + came_ref[part, :]


def halved(mine, came, bit):
    rows, width = mine.shape
    shape = jax.ShapeDtypeStruct((rows // 2, width), jnp.float32)
    return pl.pallas_call(
        halve_kernel,
        out_shape=[shape] * 2,
        in_specs=[pl.BlockSpec(memory_space=pltpu.SMEM)] + [pl.BlockSpec(memory_space=pltpu.VMEM)] * 2,
        out_specs=[pl.BlockSpec(memory_space=pltpu.VMEM)] * 2,
        compiler_params=pltpu.CompilerParams(vmem_limit_bytes=SUM_BYTES),
        cost_estimate=FREE,
    )(bit, mine, came)


def flipped_along(value, axis, flip):
    count = lax.axis_size(axis)
    return lax.ppermute(value, axis, [(source, source ^ flip[source % 2]) for source in range(count)])


def exchanged_sum(parts, bits, flips, gates=()):
    stages = []
    for level in range(1, len(bits)):
        keep, send = parts
        came = flipped_along(send, "virt", flips[level - 1])
        if level in gates:
            came = after(came, gates[level])
        parts = halved(keep, came, bits[level]) if level < len(bits) - 1 else [keep + came]
        stages.append(parts[0])
    return (parts[0], flipped_along(parts[0], "virt", flips[-1])), stages


def cut_kernel(boxes, source_ref, *refs):
    copies = []
    for index, (rows, columns) in enumerate(boxes):
        part = (rows[1] - rows[0]) // DEPTH_CUTS
        for low in range(0, rows[1] - rows[0], part):
            source = source_ref.at[rows[0] + low : rows[0] + low + part, columns[0] : columns[1]]
            target = refs[index].at[low : low + part, :]
            copies.append(pltpu.make_async_copy(source, target, refs[-1].at[len(copies)]))
    for copy in copies:
        copy.start()
    for copy in copies:
        copy.wait()


def cut_out(source, boxes):
    if any(edge % LANES for _, columns in boxes for edge in columns):
        return [source[rows[0] : rows[1], columns[0] : columns[1]] for rows, columns in boxes]
    return pl.pallas_call(
        functools.partial(cut_kernel, boxes),
        out_shape=[jax.ShapeDtypeStruct((r[1] - r[0], c[1] - c[0]), source.dtype) for r, c in boxes],
        in_specs=[pl.BlockSpec(memory_space=pl.ANY)],
        out_specs=[WHOLE] * len(boxes),
        scratch_shapes=[pltpu.SemaphoreType.DMA((DEPTH_CUTS * len(boxes),))],
        compiler_params=pltpu.CompilerParams(vmem_limit_bytes=CUT_BYTES),
        cost_estimate=FREE,
    )(source)


def last_kernel(width, starts, where_ref, rows_ref, virt_ref, occ_ref, *refs):
    blocks, (out_ref, both_ref, tall_ref, turned_ref) = refs[:-4], refs[-4:]
    rows = out_ref.shape[0]
    for index, start in enumerate(starts):
        value = blocks[index][...]
        if index == len(starts) - 1:
            value = value + blocks[index + 1][...]
        columns = out_ref.shape[1] // 2
        side = where_ref[1] if start < columns else 1 - where_ref[1]
        place = pl.multiple_of(side * columns + start % columns, LANES)
        both_ref[:, pl.ds(place, value.shape[1])] = value
    upper = where_ref[0]
    mine = both_ref[pl.ds(pl.multiple_of(upper * rows, rows), rows), :]
    other = both_ref[pl.ds(pl.multiple_of((1 - upper) * rows, rows), rows), :]
    chosen = (rows_ref[...] == lax.broadcasted_iota(jnp.int32, (rows, rows), 1)).astype(jnp.float32)
    flipped = jnp.dot(chosen, other, precision=lax.Precision.HIGHEST, preferred_element_type=jnp.float32)
    tall_ref[...] = flipped.T
    for b in range(width):
        turned_ref[b * width : (b + 1) * width, :] = tall_ref[pl.ds(b, width, stride=width), :]
    out_ref[...] = (mine + turned_ref[...].T) / (virt_ref[...] - occ_ref[...])


def last_steps(blocks, where, local_rows, virt_sum, occ_sum, width):
    rows = occ_sum.shape[0]
    columns = virt_sum.shape[0]
    starts, start = [], 0
    for block in blocks[:-1]:
        starts.append(start)
        start += block.shape[1]
    return pl.pallas_call(
        functools.partial(last_kernel, width, starts),
        out_shape=jax.ShapeDtypeStruct((rows, columns), jnp.float32),
        in_specs=[pl.BlockSpec(memory_space=pltpu.SMEM)] + [WHOLE] * (3 + len(blocks)),
        out_specs=WHOLE,
        scratch_shapes=[
            pltpu.VMEM((2 * rows, columns), jnp.float32),
            pltpu.VMEM((columns, rows), jnp.float32),
            pltpu.VMEM((columns, rows), jnp.float32),
        ],
        compiler_params=pltpu.CompilerParams(vmem_limit_bytes=SUM_BYTES),
        cost_estimate=FREE,
    )(where, local_rows.reshape(rows, 1), virt_sum.reshape(1, columns), occ_sum.reshape(rows, 1), *blocks)


def per_device(amplitudes, integrals, occ_pairs, partners, virt_list, eps_occ, eps_virt):
    width = virt_list.shape[0]
    count = lax.axis_size("pair")
    size = lax.axis_size("virt")
    rows = amplitudes.shape[0] // size
    cuts = column_cuts(integrals.shape[1])
    me = lax.axis_index("virt").astype(jnp.int32)
    levels = size.bit_length() - 1
    steps = [list(range(1, levels)), list(range(1, levels))]
    if levels > 3:
        steps[1][0:2] = [2, 1]
    own_bits = [(me >> level) & 1 for level in range(levels)]
    bits = [own_bits[0]] + [jnp.where(own_bits[0] == 1, own_bits[odd], own_bits[even]) for even, odd in zip(*steps)]
    bits = [bit.reshape(1) for bit in bits]
    flips = [[1, 1]] + [[1 << even, 1 << odd] for even, odd in zip(*steps)]
    order = [
        tuple(sum(((place >> (levels - 2 - index)) & 1) << level for index, level in enumerate(taken)) for taken in steps)
        for place in range(size // 2)
    ]
    upper = me >= size // 2

    def sent(piece):
        return [passed_along(piece, "pair", -shift) for shift in range(1, count)]

    depth = integrals.shape[0]
    late = depth // DEPTH_CUTS * (DEPTH_CUTS - 1)
    (first,) = cut_out(integrals, [((0, depth), cuts[0])])
    rest = after(integrals, first)
    boxes = [((0, depth), cut) for cut in cuts[1:-1]] + [((0, late), cuts[-1]), ((late, depth), cuts[-1])]
    pieces = [first, *cut_out(rest, boxes)]
    in_flight = [sent(pieces[0]), sent(pieces[1])]
    own_product = multiplied(amplitudes, after(rest, pieces), bits[0], order, splits=OWN_SPLITS)
    own_sums = [jnp.add(*exchanged_sum(own_product[2 * part : 2 * part + 2], bits, flips)[0]) for part in range(OWN_SPLITS)]
    sums = [own_sums] + [[] for _ in range(1, count)]
    in_flight += [sent(after(piece, own_sums)) for piece in pieces[2:]]
    earlier, gates = own_sums, {}
    for step in range(len(pieces)):
        arrived, earlier = lax.optimization_barrier((in_flight[step], earlier))
        if step == len(pieces) - 2:
            bases = [whole_plain(amplitudes, columns) for columns in arrived]
            earlier = (stages[2], bases)
            continue
        for shift in range(1, count):
            if step < len(cuts) - 1:
                product = multiplied(amplitudes, arrived[shift - 1], bits[0], order)
            else:
                product = whole_multiplied(amplitudes, arrived[shift - 1], bits[0], order, late, bases[shift - 1])
            terms, stages = exchanged_sum(product, bits, flips, gates)
            total = jnp.add(*terms)
            sums[shift].append(total)
            earlier, gates = stages[2] if step < len(cuts) - 2 else stages[0], {2: total}

    occ_ids = jnp.arange(eps_occ.shape[0], dtype=jnp.int32)
    occ_match = occ_pairs[:, :, None] == occ_ids[None, None, :]
    occ_sum = jnp.sum(jnp.where(occ_match, eps_occ[None, None, :], 0.0), axis=(1, 2))
    virt_ids = jnp.arange(eps_virt.shape[0], dtype=jnp.int32)
    virt_match = virt_list[:, None] == virt_ids[None, :]
    virt_energy = jnp.sum(jnp.where(virt_match, eps_virt[None, :], 0.0), axis=1)
    virt_sum = (virt_energy[:, None] + virt_energy[None, :]).reshape(-1)
    if count == 2 and all(block.shape[1] % LANES == 0 for parts in sums for block in parts):
        where = jnp.stack([upper.astype(jnp.int32), lax.axis_index("pair").astype(jnp.int32)])
        blocks = [*sums[0], *sums[1][:-1], *terms]
        return last_steps(blocks, where, partners % rows, virt_sum, occ_sum, width)
    both = in_column_order([jnp.concatenate(parts, axis=1) for parts in sums], count)
    mine = jnp.where(upper, both[rows:], both[:rows])
    other = jnp.where(upper, both[:rows], both[rows:])
    flipped = jnp.take(other, partners % mine.shape[0], axis=0)
    total = mine + transpose_block(flipped, width)

    denominator = virt_sum[None, :] - occ_sum[:, None]
    return total / denominator


def solution(mesh):
    placed = (
        P("pair", "virt"),
        P("virt", "pair"),
        P(("pair", "virt"), None),
        P(("pair", "virt")),
        P(),
        P(),
        P(),
    )
    return jax.shard_map(
        per_device, mesh=mesh, in_specs=placed, out_specs=P(("pair", "virt"), None), check_vma=False
    )
```

```python
import functools

import jax
import jax.numpy as jnp
from jax import lax
from jax.experimental import pallas as pl
from jax.experimental.pallas import tpu as pltpu
from jax.sharding import PartitionSpec as P

LANES = 128
DEPTH_CUTS = 4
DEPTH_PART = 1024
LATE_GATE = 3
ROW_CUTS = 1
FREE = pl.CostEstimate(flops=0, bytes_accessed=0, transcendentals=0)
OWN_SPLITS = 2
PRODUCT_BYTES = 51 * 1024 * 1024
WHOLE_BYTES = 24 * 1024 * 1024
CUT_BYTES = 56 * 1024 * 1024
SUM_BYTES = 8 * 1024 * 1024


WHOLE = pl.BlockSpec(memory_space=pltpu.VMEM)


def passed_along(value, axis, steps):
    count = lax.axis_size(axis)
    pairs = [(source, (source + steps) % count) for source in range(count)]
    return lax.ppermute(value, axis, pairs)


def transpose_block(values, width):
    count = values.shape[0]
    return values.reshape(count, width, width).transpose(0, 2, 1).reshape(count, width * width)


def column_cuts(columns):
    half, quarter = columns // 2, columns // 4
    return [(0, half), (half, half + quarter), (half + quarter, columns)]


def after(value, earlier):
    return lax.optimization_barrier((value, earlier))[0]


def in_column_order(blocks, count):
    own = lax.axis_index("pair")
    ordered = []
    for place in range(count):
        block = blocks[place]
        for index in range(1, count):
            block = jnp.where(own == index, blocks[(place - index) % count], block)
        ordered.append(block)
    return jnp.concatenate(ordered, axis=1)


def add_product(a_refs, b_ref, total_ref, base_ref):
    columns = b_ref[...]
    rows = a_refs[0].shape[0]
    for index, a_ref in enumerate(a_refs):
        part = slice(index * rows, (index + 1) * rows)
        term = jnp.dot(a_ref[...], columns, preferred_element_type=jnp.float32)

        @pl.when(pl.program_id(0) == 0)
        def _():
            total_ref[part, :] = term if base_ref is None else term + base_ref[part, :]

        @pl.when(pl.program_id(0) > 0)
        def _():
            total_ref[part, :] += term


def row_blocks(rows, part, first):
    return [pl.BlockSpec((rows // ROW_CUTS, part), lambda k, j=j: (j, k + first)) for j in range(ROW_CUTS)]


def product_cost(rows, columns):
    depth, width = columns.shape
    return pl.CostEstimate(flops=2 * rows * depth * width, bytes_accessed=2 * rows * depth, transcendentals=0)


def product_kernel(steps, order, splits, has_base, bit_ref, *refs):
    a_refs, b_ref = refs[:ROW_CUTS], refs[ROW_CUTS]
    base_ref = refs[ROW_CUTS + 1] if has_base else None
    out_refs, total_ref = refs[-1 - 2 * splits : -1], refs[-1]
    step = pl.program_id(0)
    add_product(a_refs, b_ref, total_ref, base_ref)

    @pl.when(step == steps - 1)
    def _():
        rows, width = out_refs[0].shape
        rows = rows // len(order)
        for index, out_ref in enumerate(out_refs):
            bit = 1 - bit_ref[0] if index % 2 else bit_ref[0]
            columns = slice(index // 2 * width, (index // 2 + 1) * width)
            for place, (even, odd) in enumerate(order):
                start = pl.multiple_of((even + bit * (odd - even + 1)) * rows, rows)
                out_ref[place * rows : (place + 1) * rows, :] = total_ref[pl.ds(start, rows), columns]


def multiplied(amplitudes, columns, bit, order, first=0, base=None, splits=1):
    rows, depth = amplitudes.shape
    width = columns.shape[1]
    part = depth // DEPTH_CUTS
    steps = columns.shape[0] // part
    shape = jax.ShapeDtypeStruct((rows // 2, width // splits), jnp.float32)
    bases = [] if base is None else [base]
    return pl.pallas_call(
        functools.partial(product_kernel, steps, order, splits, base is not None),
        grid=(steps,),
        out_shape=[shape] * (2 * splits),
        in_specs=[
            pl.BlockSpec(memory_space=pltpu.SMEM),
            *row_blocks(rows, part, first),
            pl.BlockSpec((part, width), lambda k: (k, 0)),
        ]
        + [pl.BlockSpec((rows, width), lambda k: (0, 0)) for _ in bases],
        out_specs=[pl.BlockSpec(shape.shape, lambda k: (0, 0))] * (2 * splits),
        scratch_shapes=[pltpu.VMEM((rows, width), jnp.float32)],
        compiler_params=pltpu.CompilerParams(vmem_limit_bytes=PRODUCT_BYTES),
        cost_estimate=product_cost(rows, columns) if splits == 1 else FREE,
    )(bit, *[amplitudes] * ROW_CUTS, columns, *bases)


def add_whole(a_ref, b_ref, total_ref, first, base_ref):
    depth = b_ref.shape[0]
    part = min(depth, DEPTH_PART)
    for low in range(0, depth, part):
        term = jnp.dot(a_ref[:, first + low : first + low + part], b_ref[low : low + part, :], preferred_element_type=jnp.float32)
        if low > 0:
            total_ref[...] += term
        else:
            total_ref[...] = term if base_ref is None else base_ref[...] + term


def whole_kernel(order, first, has_base, bit_ref, a_ref, b_ref, *refs):
    keep_ref, send_ref, total_ref = refs[-3:]
    add_whole(a_ref, b_ref, total_ref, first, refs[0] if has_base else None)
    rows = keep_ref.shape[0] // len(order)
    for out_ref, bit in ((keep_ref, bit_ref[0]), (send_ref, 1 - bit_ref[0])):
        for place, (even, odd) in enumerate(order):
            start = pl.multiple_of((even + bit * (odd - even + 1)) * rows, rows)
            out_ref[place * rows : (place + 1) * rows, :] = total_ref[pl.ds(start, rows), :]


def whole_multiplied(amplitudes, columns, bit, order, first=0, base=None):
    rows = amplitudes.shape[0]
    width = columns.shape[1]
    bases = [] if base is None else [base]
    return pl.pallas_call(
        functools.partial(whole_kernel, order, first, base is not None),
        out_shape=[jax.ShapeDtypeStruct((rows // 2, width), jnp.float32)] * 2,
        in_specs=[pl.BlockSpec(memory_space=pltpu.SMEM)] + [WHOLE] * (2 + len(bases)),
        out_specs=[WHOLE] * 2,
        scratch_shapes=[pltpu.VMEM((rows, width), jnp.float32)],
        compiler_params=pltpu.CompilerParams(vmem_limit_bytes=WHOLE_BYTES),
        cost_estimate=product_cost(rows, columns),
    )(bit, amplitudes, columns, *bases)


def whole_plain_kernel(a_ref, b_ref, out_ref):
    add_whole(a_ref, b_ref, out_ref, 0, None)


def whole_plain(amplitudes, columns):
    rows = amplitudes.shape[0]
    return pl.pallas_call(
        whole_plain_kernel,
        out_shape=jax.ShapeDtypeStruct((rows, columns.shape[1]), jnp.float32),
        in_specs=[WHOLE] * 2,
        out_specs=WHOLE,
        compiler_params=pltpu.CompilerParams(vmem_limit_bytes=WHOLE_BYTES),
        cost_estimate=product_cost(rows, columns),
    )(amplitudes, columns)


def halve_kernel(bit_ref, mine_ref, came_ref, keep_ref, send_ref):
    rows = keep_ref.shape[0]
    for out_ref, bit in ((keep_ref, bit_ref[0]), (send_ref, 1 - bit_ref[0])):
        part = pl.ds(pl.multiple_of(bit * rows, rows), rows)
        out_ref[...] = mine_ref[part, :] + came_ref[part, :]


def halved(mine, came, bit):
    rows, width = mine.shape
    shape = jax.ShapeDtypeStruct((rows // 2, width), jnp.float32)
    return pl.pallas_call(
        halve_kernel,
        out_shape=[shape] * 2,
        in_specs=[pl.BlockSpec(memory_space=pltpu.SMEM)] + [pl.BlockSpec(memory_space=pltpu.VMEM)] * 2,
        out_specs=[pl.BlockSpec(memory_space=pltpu.VMEM)] * 2,
        compiler_params=pltpu.CompilerParams(vmem_limit_bytes=SUM_BYTES),
        cost_estimate=FREE,
    )(bit, mine, came)


def flipped_along(value, axis, flip):
    count = lax.axis_size(axis)
    return lax.ppermute(value, axis, [(source, source ^ flip[source % 2]) for source in range(count)])


def exchanged_sum(parts, bits, flips, gates=()):
    stages = []
    for level in range(1, len(bits)):
        keep, send = parts
        came = flipped_along(send, "virt", flips[level - 1])
        if level in gates:
            came = after(came, gates[level](stages))
        parts = halved(keep, came, bits[level]) if level < len(bits) - 1 else [keep + came]
        stages.append(parts[0])
    return parts[0], stages


def cut_kernel(boxes, source_ref, *refs):
    copies = []
    for index, (rows, columns) in enumerate(boxes):
        part = (rows[1] - rows[0]) // DEPTH_CUTS
        for low in range(0, rows[1] - rows[0], part):
            source = source_ref.at[rows[0] + low : rows[0] + low + part, columns[0] : columns[1]]
            target = refs[index].at[low : low + part, :]
            copies.append(pltpu.make_async_copy(source, target, refs[-1].at[len(copies)]))
    for copy in copies:
        copy.start()
    for copy in copies:
        copy.wait()


def cut_out(source, boxes):
    if any(edge % LANES for _, columns in boxes for edge in columns):
        return [source[rows[0] : rows[1], columns[0] : columns[1]] for rows, columns in boxes]
    return pl.pallas_call(
        functools.partial(cut_kernel, boxes),
        out_shape=[jax.ShapeDtypeStruct((r[1] - r[0], c[1] - c[0]), source.dtype) for r, c in boxes],
        in_specs=[pl.BlockSpec(memory_space=pl.ANY)],
        out_specs=[WHOLE] * len(boxes),
        scratch_shapes=[pltpu.SemaphoreType.DMA((DEPTH_CUTS * len(boxes),))],
        compiler_params=pltpu.CompilerParams(vmem_limit_bytes=CUT_BYTES),
        cost_estimate=FREE,
    )(source)


def last_kernel(width, starts, where_ref, rows_ref, virt_ref, occ_ref, *refs):
    blocks, (out_ref, both_ref, tall_ref, turned_ref) = refs[:-4], refs[-4:]
    rows = out_ref.shape[0]
    for index, start in enumerate(starts):
        value = blocks[index][...]
        if index == len(starts) - 1:
            value = value + blocks[index + 1][...]
        columns = out_ref.shape[1] // 2
        side = where_ref[1] if start < columns else 1 - where_ref[1]
        place = pl.multiple_of(side * columns + start % columns, LANES)
        both_ref[:, pl.ds(place, value.shape[1])] = value
    upper = where_ref[0]
    mine = both_ref[pl.ds(pl.multiple_of(upper * rows, rows), rows), :]
    other = both_ref[pl.ds(pl.multiple_of((1 - upper) * rows, rows), rows), :]
    chosen = (rows_ref[...] == lax.broadcasted_iota(jnp.int32, (rows, rows), 1)).astype(jnp.float32)
    flipped = jnp.dot(chosen, other, precision=lax.Precision.HIGHEST, preferred_element_type=jnp.float32)
    tall_ref[...] = flipped.T
    for b in range(width):
        turned_ref[b * width : (b + 1) * width, :] = tall_ref[pl.ds(b, width, stride=width), :]
    out_ref[...] = (mine + turned_ref[...].T) / (virt_ref[...] - occ_ref[...])


def last_steps(blocks, where, local_rows, virt_sum, occ_sum, width):
    rows = occ_sum.shape[0]
    columns = virt_sum.shape[0]
    starts, start = [], 0
    for block in blocks[:-1]:
        starts.append(start)
        start += block.shape[1]
    return pl.pallas_call(
        functools.partial(last_kernel, width, starts),
        out_shape=jax.ShapeDtypeStruct((rows, columns), jnp.float32),
        in_specs=[pl.BlockSpec(memory_space=pltpu.SMEM)] + [WHOLE] * (3 + len(blocks)),
        out_specs=WHOLE,
        scratch_shapes=[
            pltpu.VMEM((2 * rows, columns), jnp.float32),
            pltpu.VMEM((columns, rows), jnp.float32),
            pltpu.VMEM((columns, rows), jnp.float32),
        ],
        compiler_params=pltpu.CompilerParams(vmem_limit_bytes=SUM_BYTES),
        cost_estimate=FREE,
    )(where, local_rows.reshape(rows, 1), virt_sum.reshape(1, columns), occ_sum.reshape(rows, 1), *blocks)


def both_halves(part, flips):
    return part + flipped_along(part, "virt", flips[-1])


def per_device(amplitudes, integrals, occ_pairs, partners, virt_list, eps_occ, eps_virt):
    width = virt_list.shape[0]
    count = lax.axis_size("pair")
    size = lax.axis_size("virt")
    rows = amplitudes.shape[0] // size
    cuts = column_cuts(integrals.shape[1])
    me = lax.axis_index("virt").astype(jnp.int32)
    levels = size.bit_length() - 1
    steps = [list(range(1, levels)), list(range(1, levels))]
    if levels > 3:
        steps[1][0:2] = [2, 1]
    own_bits = [(me >> level) & 1 for level in range(levels)]
    bits = [own_bits[0]] + [jnp.where(own_bits[0] == 1, own_bits[odd], own_bits[even]) for even, odd in zip(*steps)]
    bits = [bit.reshape(1) for bit in bits]
    flips = [[1, 1]] + [[1 << even, 1 << odd] for even, odd in zip(*steps)]
    order = [
        tuple(sum(((place >> (levels - 2 - index)) & 1) << level for index, level in enumerate(taken)) for taken in steps)
        for place in range(size // 2)
    ]
    upper = me >= size // 2

    def sent(piece):
        return [passed_along(piece, "pair", -shift) for shift in range(1, count)]

    depth = integrals.shape[0]
    late = depth // DEPTH_CUTS * (DEPTH_CUTS - 1)
    (first,) = cut_out(integrals, [((0, depth), cuts[0])])
    rest = after(integrals, first)
    boxes = [((0, depth), cut) for cut in cuts[1:-1]] + [((0, late), cuts[-1]), ((late, depth), cuts[-1])]
    pieces = [first, *cut_out(rest, boxes)]
    in_flight = [sent(pieces[0]), sent(pieces[1])]
    own_product = multiplied(amplitudes, after(rest, pieces), bits[0], order, splits=OWN_SPLITS)
    own_sums = [both_halves(exchanged_sum(own_product[2 * part : 2 * part + 2], bits, flips)[0], flips) for part in range(OWN_SPLITS)]
    sums = [own_sums] + [[] for _ in range(1, count)]
    in_flight += [sent(after(piece, own_sums)) for piece in pieces[2:]]
    later = after(amplitudes, own_product)
    first_part, last_part = later[:, :late], later[:, late:]
    earlier, gates = (own_sums, first_part, last_part), {}
    for step in range(len(pieces)):
        arrived, earlier = lax.optimization_barrier((in_flight[step], earlier))
        if step == len(pieces) - 2:
            bases = [whole_plain(first_part, columns) for columns in arrived]
            earlier = (stages[2], bases)
            continue
        for shift in range(1, count):
            if step < len(cuts) - 1:
                product = multiplied(amplitudes, arrived[shift - 1], bits[0], order)
            else:
                product = whole_multiplied(last_part, arrived[shift - 1], bits[0], order, 0, bases[shift - 1])
            part, stages = exchanged_sum(product, bits, flips, gates)
            if step == 0 or (step < len(cuts) - 1 and shift < count - 1):
                total = both_halves(part, flips)
                sums[shift].append(total)
                earlier, gates = stages[2], {2: lambda _, total=total: total}
            elif step < len(cuts) - 1:

                def finished(later, part=part, shift=shift):
                    total = both_halves(after(part, later[0]), flips)
                    sums[shift].append(total)
                    return total

                earlier, gates = stages[0], {LATE_GATE: finished}
            else:
                terms = part, flipped_along(part, "virt", flips[-1])
                sums[shift].append(jnp.add(*terms))
                gates = {}

    occ_ids = jnp.arange(eps_occ.shape[0], dtype=jnp.int32)
    occ_match = occ_pairs[:, :, None] == occ_ids[None, None, :]
    occ_sum = jnp.sum(jnp.where(occ_match, eps_occ[None, None, :], 0.0), axis=(1, 2))
    virt_ids = jnp.arange(eps_virt.shape[0], dtype=jnp.int32)
    virt_match = virt_list[:, None] == virt_ids[None, :]
    virt_energy = jnp.sum(jnp.where(virt_match, eps_virt[None, :], 0.0), axis=1)
    virt_sum = (virt_energy[:, None] + virt_energy[None, :]).reshape(-1)
    if count == 2 and all(block.shape[1] % LANES == 0 for parts in sums for block in parts):
        where = jnp.stack([upper.astype(jnp.int32), lax.axis_index("pair").astype(jnp.int32)])
        blocks = [*sums[0], *sums[1][:-1], *terms]
        return last_steps(blocks, where, partners % rows, virt_sum, occ_sum, width)
    both = in_column_order([jnp.concatenate(parts, axis=1) for parts in sums], count)
    mine = jnp.where(upper, both[rows:], both[:rows])
    other = jnp.where(upper, both[:rows], both[rows:])
    flipped = jnp.take(other, partners % mine.shape[0], axis=0)
    total = mine + transpose_block(flipped, width)

    denominator = virt_sum[None, :] - occ_sum[:, None]
    return total / denominator


def solution(mesh):
    placed = (
        P("pair", "virt"),
        P("virt", "pair"),
        P(("pair", "virt"), None),
        P(("pair", "virt")),
        P(),
        P(),
        P(),
    )
    return jax.shard_map(
        per_device, mesh=mesh, in_specs=placed, out_specs=P(("pair", "virt"), None), check_vma=False
    )
```

```python
import functools

import jax
import jax.numpy as jnp
from jax import lax
from jax.experimental import pallas as pl
from jax.experimental.pallas import tpu as pltpu
from jax.sharding import PartitionSpec as P

LANES = 128
DEPTH_CUTS = 4
CUT_PARTS = 16
DEPTH_PART = 1024
LATE_GATE = 3
ROW_CUTS = 1
FREE = pl.CostEstimate(flops=0, bytes_accessed=0, transcendentals=0)
OWN_SPLITS = 2
PRODUCT_BYTES = 51 * 1024 * 1024
WHOLE_BYTES = 24 * 1024 * 1024
CUT_BYTES = 56 * 1024 * 1024
SUM_BYTES = 8 * 1024 * 1024


WHOLE = pl.BlockSpec(memory_space=pltpu.VMEM)


def passed_along(value, axis, steps):
    count = lax.axis_size(axis)
    pairs = [(source, (source + steps) % count) for source in range(count)]
    return lax.ppermute(value, axis, pairs)


def transpose_block(values, width):
    count = values.shape[0]
    return values.reshape(count, width, width).transpose(0, 2, 1).reshape(count, width * width)


def column_cuts(columns):
    half, quarter = columns // 2, columns // 4
    return [(0, half), (half, half + quarter), (half + quarter, columns)]


def after(value, earlier):
    return lax.optimization_barrier((value, earlier))[0]


def in_column_order(blocks, count):
    own = lax.axis_index("pair")
    ordered = []
    for place in range(count):
        block = blocks[place]
        for index in range(1, count):
            block = jnp.where(own == index, blocks[(place - index) % count], block)
        ordered.append(block)
    return jnp.concatenate(ordered, axis=1)


def add_product(a_refs, b_ref, total_ref, base_ref):
    columns = b_ref[...]
    rows = a_refs[0].shape[0]
    for index, a_ref in enumerate(a_refs):
        part = slice(index * rows, (index + 1) * rows)
        term = jnp.dot(a_ref[...], columns, preferred_element_type=jnp.float32)

        @pl.when(pl.program_id(0) == 0)
        def _():
            total_ref[part, :] = term if base_ref is None else term + base_ref[part, :]

        @pl.when(pl.program_id(0) > 0)
        def _():
            total_ref[part, :] += term


def row_blocks(rows, part, first):
    return [pl.BlockSpec((rows // ROW_CUTS, part), lambda k, j=j: (j, k + first)) for j in range(ROW_CUTS)]


def product_cost(rows, columns):
    depth, width = columns.shape
    return pl.CostEstimate(flops=2 * rows * depth * width, bytes_accessed=2 * rows * depth, transcendentals=0)


def product_kernel(steps, order, splits, has_base, bit_ref, *refs):
    a_refs, b_ref = refs[:ROW_CUTS], refs[ROW_CUTS]
    base_ref = refs[ROW_CUTS + 1] if has_base else None
    out_refs, total_ref = refs[-1 - 2 * splits : -1], refs[-1]
    step = pl.program_id(0)
    add_product(a_refs, b_ref, total_ref, base_ref)

    @pl.when(step == steps - 1)
    def _():
        rows, width = out_refs[0].shape
        rows = rows // len(order)
        for index, out_ref in enumerate(out_refs):
            bit = 1 - bit_ref[0] if index % 2 else bit_ref[0]
            columns = slice(index // 2 * width, (index // 2 + 1) * width)
            for place, (even, odd) in enumerate(order):
                start = pl.multiple_of((even + bit * (odd - even + 1)) * rows, rows)
                out_ref[place * rows : (place + 1) * rows, :] = total_ref[pl.ds(start, rows), columns]


def multiplied(amplitudes, columns, bit, order, first=0, base=None, splits=1):
    rows, depth = amplitudes.shape
    width = columns.shape[1]
    part = depth // DEPTH_CUTS
    steps = columns.shape[0] // part
    shape = jax.ShapeDtypeStruct((rows // 2, width // splits), jnp.float32)
    bases = [] if base is None else [base]
    return pl.pallas_call(
        functools.partial(product_kernel, steps, order, splits, base is not None),
        grid=(steps,),
        out_shape=[shape] * (2 * splits),
        in_specs=[
            pl.BlockSpec(memory_space=pltpu.SMEM),
            *row_blocks(rows, part, first),
            pl.BlockSpec((part, width), lambda k: (k, 0)),
        ]
        + [pl.BlockSpec((rows, width), lambda k: (0, 0)) for _ in bases],
        out_specs=[pl.BlockSpec(shape.shape, lambda k: (0, 0))] * (2 * splits),
        scratch_shapes=[pltpu.VMEM((rows, width), jnp.float32)],
        compiler_params=pltpu.CompilerParams(vmem_limit_bytes=PRODUCT_BYTES),
        cost_estimate=product_cost(rows, columns) if splits == 1 else FREE,
    )(bit, *[amplitudes] * ROW_CUTS, columns, *bases)


def add_whole(a_ref, b_ref, total_ref, first, base_ref):
    depth = b_ref.shape[0]
    part = min(depth, DEPTH_PART)
    for low in range(0, depth, part):
        term = jnp.dot(a_ref[:, first + low : first + low + part], b_ref[low : low + part, :], preferred_element_type=jnp.float32)
        if low > 0:
            total_ref[...] += term
        else:
            total_ref[...] = term if base_ref is None else base_ref[...] + term


def whole_kernel(order, first, has_base, bit_ref, a_ref, b_ref, *refs):
    keep_ref, send_ref, total_ref = refs[-3:]
    add_whole(a_ref, b_ref, total_ref, first, refs[0] if has_base else None)
    rows = keep_ref.shape[0] // len(order)
    for out_ref, bit in ((keep_ref, bit_ref[0]), (send_ref, 1 - bit_ref[0])):
        for place, (even, odd) in enumerate(order):
            start = pl.multiple_of((even + bit * (odd - even + 1)) * rows, rows)
            out_ref[place * rows : (place + 1) * rows, :] = total_ref[pl.ds(start, rows), :]


def whole_multiplied(amplitudes, columns, bit, order, first=0, base=None):
    rows = amplitudes.shape[0]
    width = columns.shape[1]
    bases = [] if base is None else [base]
    return pl.pallas_call(
        functools.partial(whole_kernel, order, first, base is not None),
        out_shape=[jax.ShapeDtypeStruct((rows // 2, width), jnp.float32)] * 2,
        in_specs=[pl.BlockSpec(memory_space=pltpu.SMEM)] + [WHOLE] * (2 + len(bases)),
        out_specs=[WHOLE] * 2,
        scratch_shapes=[pltpu.VMEM((rows, width), jnp.float32)],
        compiler_params=pltpu.CompilerParams(vmem_limit_bytes=WHOLE_BYTES),
        cost_estimate=product_cost(rows, columns),
    )(bit, amplitudes, columns, *bases)


def whole_plain_kernel(a_ref, b_ref, out_ref):
    add_whole(a_ref, b_ref, out_ref, 0, None)


def whole_plain(amplitudes, columns):
    rows = amplitudes.shape[0]
    return pl.pallas_call(
        whole_plain_kernel,
        out_shape=jax.ShapeDtypeStruct((rows, columns.shape[1]), jnp.float32),
        in_specs=[WHOLE] * 2,
        out_specs=WHOLE,
        compiler_params=pltpu.CompilerParams(vmem_limit_bytes=WHOLE_BYTES),
        cost_estimate=product_cost(rows, columns),
    )(amplitudes, columns)


def halve_kernel(bit_ref, mine_ref, came_ref, keep_ref, send_ref):
    rows = keep_ref.shape[0]
    for out_ref, bit in ((keep_ref, bit_ref[0]), (send_ref, 1 - bit_ref[0])):
        part = pl.ds(pl.multiple_of(bit * rows, rows), rows)
        out_ref[...] = mine_ref[part, :] + came_ref[part, :]


def halved(mine, came, bit):
    rows, width = mine.shape
    shape = jax.ShapeDtypeStruct((rows // 2, width), jnp.float32)
    return pl.pallas_call(
        halve_kernel,
        out_shape=[shape] * 2,
        in_specs=[pl.BlockSpec(memory_space=pltpu.SMEM)] + [pl.BlockSpec(memory_space=pltpu.VMEM)] * 2,
        out_specs=[pl.BlockSpec(memory_space=pltpu.VMEM)] * 2,
        compiler_params=pltpu.CompilerParams(vmem_limit_bytes=SUM_BYTES),
        cost_estimate=FREE,
    )(bit, mine, came)


def flipped_along(value, axis, flip):
    count = lax.axis_size(axis)
    return lax.ppermute(value, axis, [(source, source ^ flip[source % 2]) for source in range(count)])


def exchanged_sum(parts, bits, flips, gates=()):
    stages = []
    for level in range(1, len(bits)):
        keep, send = parts
        came = flipped_along(send, "virt", flips[level - 1])
        if level in gates:
            came = after(came, gates[level](stages))
        parts = halved(keep, came, bits[level]) if level < len(bits) - 1 else [keep + came]
        stages.append(parts[0])
    return parts[0], stages


def cut_kernel(boxes, source_ref, *refs):
    copies = []
    for index, (rows, columns) in enumerate(boxes):
        part = (rows[1] - rows[0]) // CUT_PARTS
        for low in range(0, rows[1] - rows[0], part):
            source = source_ref.at[rows[0] + low : rows[0] + low + part, columns[0] : columns[1]]
            target = refs[index].at[low : low + part, :]
            copies.append(pltpu.make_async_copy(source, target, refs[-1].at[len(copies)]))
    for copy in copies:
        copy.start()
    for copy in copies:
        copy.wait()


def cut_out(source, boxes):
    if any(edge % LANES for _, columns in boxes for edge in columns):
        return [source[rows[0] : rows[1], columns[0] : columns[1]] for rows, columns in boxes]
    return pl.pallas_call(
        functools.partial(cut_kernel, boxes),
        out_shape=[jax.ShapeDtypeStruct((r[1] - r[0], c[1] - c[0]), source.dtype) for r, c in boxes],
        in_specs=[pl.BlockSpec(memory_space=pl.ANY)],
        out_specs=[WHOLE] * len(boxes),
        scratch_shapes=[pltpu.SemaphoreType.DMA((CUT_PARTS * len(boxes),))],
        compiler_params=pltpu.CompilerParams(vmem_limit_bytes=CUT_BYTES),
        cost_estimate=FREE,
    )(source)


def last_kernel(width, starts, where_ref, rows_ref, virt_ref, occ_ref, *refs):
    blocks, (out_ref, both_ref, tall_ref, turned_ref) = refs[:-4], refs[-4:]
    rows = out_ref.shape[0]
    for index, start in enumerate(starts):
        value = blocks[index][...]
        if index == len(starts) - 1:
            value = value + blocks[index + 1][...]
        columns = out_ref.shape[1] // 2
        side = where_ref[1] if start < columns else 1 - where_ref[1]
        place = pl.multiple_of(side * columns + start % columns, LANES)
        both_ref[:, pl.ds(place, value.shape[1])] = value
    upper = where_ref[0]
    mine = both_ref[pl.ds(pl.multiple_of(upper * rows, rows), rows), :]
    other = both_ref[pl.ds(pl.multiple_of((1 - upper) * rows, rows), rows), :]
    chosen = (rows_ref[...] == lax.broadcasted_iota(jnp.int32, (rows, rows), 1)).astype(jnp.float32)
    flipped = jnp.dot(chosen, other, precision=lax.Precision.HIGHEST, preferred_element_type=jnp.float32)
    tall_ref[...] = flipped.T
    for b in range(width):
        turned_ref[b * width : (b + 1) * width, :] = tall_ref[pl.ds(b, width, stride=width), :]
    out_ref[...] = (mine + turned_ref[...].T) / (virt_ref[...] - occ_ref[...])


def last_steps(blocks, where, local_rows, virt_sum, occ_sum, width):
    rows = occ_sum.shape[0]
    columns = virt_sum.shape[0]
    starts, start = [], 0
    for block in blocks[:-1]:
        starts.append(start)
        start += block.shape[1]
    return pl.pallas_call(
        functools.partial(last_kernel, width, starts),
        out_shape=jax.ShapeDtypeStruct((rows, columns), jnp.float32),
        in_specs=[pl.BlockSpec(memory_space=pltpu.SMEM)] + [WHOLE] * (3 + len(blocks)),
        out_specs=WHOLE,
        scratch_shapes=[
            pltpu.VMEM((2 * rows, columns), jnp.float32),
            pltpu.VMEM((columns, rows), jnp.float32),
            pltpu.VMEM((columns, rows), jnp.float32),
        ],
        compiler_params=pltpu.CompilerParams(vmem_limit_bytes=SUM_BYTES),
        cost_estimate=FREE,
    )(where, local_rows.reshape(rows, 1), virt_sum.reshape(1, columns), occ_sum.reshape(rows, 1), *blocks)


def both_halves(part, flips):
    return part + flipped_along(part, "virt", flips[-1])


def per_device(amplitudes, integrals, occ_pairs, partners, virt_list, eps_occ, eps_virt):
    width = virt_list.shape[0]
    count = lax.axis_size("pair")
    size = lax.axis_size("virt")
    rows = amplitudes.shape[0] // size
    cuts = column_cuts(integrals.shape[1])
    me = lax.axis_index("virt").astype(jnp.int32)
    levels = size.bit_length() - 1
    steps = [list(range(1, levels)), list(range(1, levels))]
    if levels > 3:
        steps[1][0:2] = [2, 1]
    own_bits = [(me >> level) & 1 for level in range(levels)]
    bits = [own_bits[0]] + [jnp.where(own_bits[0] == 1, own_bits[odd], own_bits[even]) for even, odd in zip(*steps)]
    bits = [bit.reshape(1) for bit in bits]
    flips = [[1, 1]] + [[1 << even, 1 << odd] for even, odd in zip(*steps)]
    order = [
        tuple(sum(((place >> (levels - 2 - index)) & 1) << level for index, level in enumerate(taken)) for taken in steps)
        for place in range(size // 2)
    ]
    upper = me >= size // 2

    def sent(piece):
        return [passed_along(piece, "pair", -shift) for shift in range(1, count)]

    depth = integrals.shape[0]
    late = depth // DEPTH_CUTS * (DEPTH_CUTS - 1)
    (first,) = cut_out(integrals, [((0, depth), cuts[0])])
    rest = after(integrals, first)
    boxes = [((0, depth), cut) for cut in cuts[1:-1]] + [((0, late), cuts[-1]), ((late, depth), cuts[-1])]
    pieces = [first, *cut_out(rest, boxes)]
    in_flight = [sent(pieces[0]), sent(pieces[1])]
    own_product = multiplied(amplitudes, after(rest, pieces), bits[0], order, splits=OWN_SPLITS)
    own_sums = [both_halves(exchanged_sum(own_product[2 * part : 2 * part + 2], bits, flips)[0], flips) for part in range(OWN_SPLITS)]
    sums = [own_sums] + [[] for _ in range(1, count)]
    in_flight += [sent(after(piece, own_sums)) for piece in pieces[2:]]
    later = after(amplitudes, own_product)
    first_part, last_part = later[:, :late], later[:, late:]
    earlier, gates = (own_sums, first_part, last_part), {}
    for step in range(len(pieces)):
        arrived, earlier = lax.optimization_barrier((in_flight[step], earlier))
        if step == len(pieces) - 2:
            bases = [whole_plain(first_part, columns) for columns in arrived]
            earlier = (stages[2], bases)
            continue
        for shift in range(1, count):
            if step < len(cuts) - 1:
                product = multiplied(amplitudes, arrived[shift - 1], bits[0], order)
            else:
                product = whole_multiplied(last_part, arrived[shift - 1], bits[0], order, 0, bases[shift - 1])
            part, stages = exchanged_sum(product, bits, flips, gates)
            if step == 0 or (step < len(cuts) - 1 and shift < count - 1):
                total = both_halves(part, flips)
                sums[shift].append(total)
                earlier, gates = stages[2], {2: lambda _, total=total: total}
            elif step < len(cuts) - 1:

                def finished(later, part=part, shift=shift):
                    total = both_halves(after(part, later[0]), flips)
                    sums[shift].append(total)
                    return total

                earlier, gates = stages[0], {LATE_GATE: finished}
            else:
                terms = part, flipped_along(part, "virt", flips[-1])
                sums[shift].append(jnp.add(*terms))
                gates = {}

    occ_ids = jnp.arange(eps_occ.shape[0], dtype=jnp.int32)
    occ_match = occ_pairs[:, :, None] == occ_ids[None, None, :]
    occ_sum = jnp.sum(jnp.where(occ_match, eps_occ[None, None, :], 0.0), axis=(1, 2))
    virt_ids = jnp.arange(eps_virt.shape[0], dtype=jnp.int32)
    virt_match = virt_list[:, None] == virt_ids[None, :]
    virt_energy = jnp.sum(jnp.where(virt_match, eps_virt[None, :], 0.0), axis=1)
    virt_sum = (virt_energy[:, None] + virt_energy[None, :]).reshape(-1)
    if count == 2 and all(block.shape[1] % LANES == 0 for parts in sums for block in parts):
        where = jnp.stack([upper.astype(jnp.int32), lax.axis_index("pair").astype(jnp.int32)])
        blocks = [*sums[0], *sums[1][:-1], *terms]
        return last_steps(blocks, where, partners % rows, virt_sum, occ_sum, width)
    both = in_column_order([jnp.concatenate(parts, axis=1) for parts in sums], count)
    mine = jnp.where(upper, both[rows:], both[:rows])
    other = jnp.where(upper, both[:rows], both[rows:])
    flipped = jnp.take(other, partners % mine.shape[0], axis=0)
    total = mine + transpose_block(flipped, width)

    denominator = virt_sum[None, :] - occ_sum[:, None]
    return total / denominator


def solution(mesh):
    placed = (
        P("pair", "virt"),
        P("virt", "pair"),
        P(("pair", "virt"), None),
        P(("pair", "virt")),
        P(),
        P(),
        P(),
    )
    return jax.shard_map(
        per_device, mesh=mesh, in_specs=placed, out_specs=P(("pair", "virt"), None), check_vma=False
    )
```
